32 devices in a mesh: grp: 4 (over y, x), gx: 4 (over z), gy: 2 (over core).
Axes of the slice: x: 2, y: 2, z: 4, core: 2. Of those that a mesh axis runs over, the one named last changes fastest.
Arguments:
- fwd_now: float32 [3, 16, 16, 128], P(None, 'gx', 'gy'), may hold values from -6 to 6
- fwd_prev: float32 [3, 16, 16, 128], P(None, 'gx', 'gy'), may hold values from -6 to 6
- adj_now: float32 [16, 3, 16, 16, 128], P('grp', None, 'gx', 'gy'), may hold values from -6 to 6
- adj_prev: float32 [16, 3, 16, 16, 128], P('grp', None, 'gx', 'gy'), may hold values from -6 to 6
- lame_first: float32 [16, 16, 128], P('gx', 'gy'), may hold values from 0.5 to 2
- shear_mod: float32 [16, 16, 128], P('gx', 'gy'), may hold values from 0.3 to 1.2
- buoyancy: float32 [16, 16, 128], P('gx', 'gy'), may hold values from 0.5 to 1
- master_cell: int32 [1], replicated, may hold values from 0 to 32767
- master_lag: int32 [1], replicated, may hold values from 0 to 254
- master_trace: float32 [256, 3], replicated, may hold values from -96 to 96
- receiver_cell: int32 [16], P('grp'), may hold values from 0 to 32767
- receiver_lag: int32 [16], P('grp'), may hold values from 0 to 254
- receiver_trace: float32 [16, 256, 3], P('grp'), may hold values from -96 to 96
Outputs:
- adj_final: float32 [16, 3, 16, 16, 128], P('grp', None, 'gx', 'gy')
- kernels: float32 [2, 16, 16, 128], P(None, 'gx', 'gy', 'grp')
The draws below stay inside these ranges and needn't reach their ends.
Inputs may be any that keep to these rules, and one draw needn't show every extreme that they name: `receiver_cell`: cell index in the whole grid, numbered (x * 16 + y) * 128 + z. `master_cell`: cell index in the whole grid, numbered (x * 16 + y) * 128 + z.
All inputs are finite; a program needn't handle non-finite values.
Results may differ from the reference program's by a relative error of at most 0.00011.
Values sent between devices are 32-bit elements; how exact they have to be, the bound alone decides.
A program may use at most 64 MiB of HBM per device.

```python
import math
import jax
import jax.numpy as jnp
from jax import lax

NZ = 128
STEPS = 2
TRACE = 256
NX = 16
NY = 16
RCV_ALL = 16


def set_ends(entries, rng, low, largest):
    extent = entries.shape
    spot = [jax.random.randint(jax.random.fold_in(rng, axis), (), 0, extent[axis]) for axis in range(len(extent))]
    entries = entries.at[tuple(spot)].set(low)
    longest = extent.index(max(extent))
    spot[longest] = (spot[longest] + 1) % extent[longest]
    return entries.at[tuple(spot)].set(largest)


def levels(rng, extent, shards, smallest, high):
    level = 1.0
    for dim, parts in shards:
        draws = jax.random.uniform(jax.random.fold_in(jax.random.fold_in(rng, 6), dim), (parts,), jnp.float32, smallest / len(shards), high / len(shards))
        level = level * jnp.repeat(jnp.exp(draws), extent[dim] // parts).reshape((-1,) + (1,) * (len(extent) - 1 - dim))
    return level


def noise(key, shape, spread, limit, pieces=(), kind=jnp.bfloat16):
    entries = jax.random.normal(key, shape, jnp.float32) * spread
    if len(pieces) > 0:
        entries = levels(key, shape, pieces, -0.22, 0.18) * entries
    return jnp.clip(entries, min=-limit, max=limit).astype(kind)


def setup_inputs(seed: int = 0) -> dict:
    streams_of = jax.random.split(jax.random.key(seed), 14)
    fwd_now = noise(streams_of[0], (3, NX, NY, NZ), 1.0, 6.0, ((1, 4), (2, 2)), jnp.float32)
    fwd_prev = noise(streams_of[1], (3, NX, NY, NZ), 1.0, 6.0, ((1, 4), (2, 2)), jnp.float32)
    adj_now = noise(streams_of[2], (RCV_ALL, 3, NX, NY, NZ), 1.0, 6.0, ((0, 4), (2, 4), (3, 2)), jnp.float32)
    adj_prev = noise(streams_of[3], (RCV_ALL, 3, NX, NY, NZ), 1.0, 6.0, ((0, 4), (2, 4), (3, 2)), jnp.float32)
    lame_first = jnp.clip(jnp.exp(math.log(2.0) - 1.3862944 * jax.random.uniform(streams_of[4], (NX, NY, NZ), jnp.float32) ** levels(streams_of[4], (NX, NY, NZ), ((0, 4), (1, 2)), -0.2, 0.2)), 0.5, 2.0)
    shear_mod = jnp.clip(jnp.exp(math.log(1.2) - 1.3862944 * jax.random.uniform(streams_of[5], (NX, NY, NZ), jnp.float32) ** levels(streams_of[5], (NX, NY, NZ), ((0, 4), (1, 2)), -0.2, 0.2)), 0.3, 1.2)
    buoyancy = jnp.clip(jnp.exp(math.log(1.0) - 0.6931472 * jax.random.uniform(streams_of[6], (NX, NY, NZ), jnp.float32) ** levels(streams_of[6], (NX, NY, NZ), ((0, 4), (1, 2)), -0.2, 0.2)), 0.5, 1.0)
    master_cell = jax.random.randint(streams_of[7], (1,), 0, NX * NY * NZ).astype(jnp.int32)
    master_lag = jax.random.randint(streams_of[8], (1,), 0, TRACE - STEPS + 1).astype(jnp.int32)
    master_trace = noise(streams_of[9], (TRACE, 3), 16.0, 96.0, (), jnp.float32)
    receiver_cell = set_ends(jax.random.randint(streams_of[10], (RCV_ALL,), 0, NX * NY * NZ), jax.random.fold_in(streams_of[10], 1), 0, (NX * NY * NZ) - 1).astype(jnp.int32)
    receiver_lag = set_ends(jax.random.randint(streams_of[11], (RCV_ALL,), 0, TRACE - STEPS + 1), jax.random.fold_in(streams_of[11], 1), 0, TRACE - STEPS).astype(jnp.int32)
    receiver_trace = noise(streams_of[12], (RCV_ALL, TRACE, 3), 16.0, 96.0, ((0, 4),), jnp.float32)
    return {"fwd_now": fwd_now, "fwd_prev": fwd_prev, "adj_now": adj_now, "adj_prev": adj_prev, "lame_first": lame_first, "shear_mod": shear_mod, "buoyancy": buoyancy, "master_cell": master_cell, "master_lag": master_lag, "master_trace": master_trace, "receiver_cell": receiver_cell, "receiver_lag": receiver_lag, "receiver_trace": receiver_trace}


time_step_sq = 0.0625


def backward_diff(stress, axis):
    upper = stress[:, 1:, 1:, 1:]
    if axis == 1:
        lower = stress[:, :-1, 1:, 1:]
    elif axis == 2:
        lower = stress[:, 1:, :-1, 1:]
    else:
        lower = stress[:, 1:, 1:, :-1]
    return upper - lower


def stencil(padded, lame_pad, shear_pad):
    span_x = padded.shape[2] - 2
    span_y = padded.shape[3] - 2
    span_z = padded.shape[4] - 2
    anchor = padded[:, :, :span_x + 1, :span_y + 1, :span_z + 1]
    grad_x = padded[:, :, 1:, :span_y + 1, :span_z + 1] - anchor
    grad_y = padded[:, :, :span_x + 1, 1:, :span_z + 1] - anchor
    grad_z = padded[:, :, :span_x + 1, :span_y + 1, 1:] - anchor
    strain_xx = grad_x[:, 0]
    strain_yy = grad_y[:, 1]
    strain_zz = grad_z[:, 2]
    strain_xy = 0.5 * (grad_y[:, 0] + grad_x[:, 1])
    strain_xz = 0.5 * (grad_z[:, 0] + grad_x[:, 2])
    strain_yz = 0.5 * (grad_z[:, 1] + grad_y[:, 2])
    lame = lame_pad[:span_x + 1, :span_y + 1, :span_z + 1]
    shear = shear_pad[:span_x + 1, :span_y + 1, :span_z + 1]
    dilation = strain_xx + strain_yy + strain_zz
    stress_xx = lame * dilation + 2.0 * shear * strain_xx
    stress_yy = lame * dilation + 2.0 * shear * strain_yy
    stress_zz = lame * dilation + 2.0 * shear * strain_zz
    stress_xy = 2.0 * shear * strain_xy
    stress_xz = 2.0 * shear * strain_xz
    stress_yz = 2.0 * shear * strain_yz
    force_x = backward_diff(stress_xx, 1) + backward_diff(stress_xy, 2) + backward_diff(stress_xz, 3)
    force_y = backward_diff(stress_xy, 1) + backward_diff(stress_yy, 2) + backward_diff(stress_yz, 3)
    force_z = backward_diff(stress_xz, 1) + backward_diff(stress_yz, 2) + backward_diff(stress_zz, 3)
    force = jnp.stack([force_x, force_y, force_z], axis=1)
    strain = jnp.stack([strain_xx, strain_yy, strain_zz, strain_xy, strain_xz, strain_yz], axis=1)
    return force, strain[:, :, 1:, 1:, 1:]


def reference(fwd_now, fwd_prev, adj_now, adj_prev, lame_first, shear_mod, buoyancy, master_cell, master_lag, master_trace, receiver_cell, receiver_lag, receiver_trace):
    lame_pad = jnp.pad(lame_first, 1)
    shear_pad = jnp.pad(shear_mod, 1)
    weights = jnp.array([1.0, 1.0, 1.0, 2.0, 2.0, 2.0], jnp.float32)[:, None, None, None]

    def advance(current, earlier, cell, lag, trace, instant):
        padded = jnp.pad(current, ((0, 0), (1, 1), (1, 1), (1, 1)))[None]
        force, strain = stencil(padded, lame_pad, shear_pad)
        amplitude = lax.dynamic_index_in_dim(trace, lag + instant, 0, keepdims=False)
        placed = jnp.zeros((NX * NY * NZ,), jnp.float32).at[cell].add(1.0).reshape(NX, NY, NZ)
        source = amplitude[:, None, None, None] * placed[None]
        following = 2.0 * current - earlier + time_step_sq * buoyancy * (force[0] + source)
        return following, strain[0]

    master_strains = []
    current, earlier = fwd_now, fwd_prev
    for instant in range(STEPS):
        following, strain = advance(current, earlier, master_cell[0], master_lag[0], master_trace, instant)
        master_strains.append(strain)
        current, earlier = following, current

    def one_receiver(packed):
        current, earlier, cell, lag, trace = packed
        dilation_term = jnp.zeros((NX, NY, NZ), jnp.float32)
        shear_term = jnp.zeros((NX, NY, NZ), jnp.float32)
        for instant in range(STEPS):
            following, strain = advance(current, earlier, cell, lag, trace, instant)
            master = master_strains[instant]
            dilation_term = dilation_term + (master[0] + master[1] + master[2]) * (strain[0] + strain[1] + strain[2])
            shear_term = shear_term + 2.0 * jnp.sum(weights * master * strain, axis=0)
            current, earlier = following, current
        return current, dilation_term, shear_term

    finals, dilation_terms, shear_terms = lax.map(one_receiver, (adj_now, adj_prev, receiver_cell, receiver_lag, receiver_trace))
    scale_out = 1.0 / (STEPS * RCV_ALL)
    kernels = jnp.stack([jnp.sum(dilation_terms, axis=0), jnp.sum(shear_terms, axis=0)]) * scale_out
    return finals, kernels
```

```python
import functools

import jax
import jax.numpy as jnp
from jax import lax
from jax.experimental import pallas as pl
from jax.experimental.pallas import tpu as pltpu
from jax.sharding import PartitionSpec as P

STEPS = 2
MESH = pl.DeviceIdType.MESH

time_step_sq = 0.0625


def kernel(
    sizes,
    master_cell,
    master_lag,
    master_trace,
    receiver_cell,
    receiver_lag,
    receiver_trace,
    fwd_now,
    fwd_prev,
    adj_now,
    adj_prev,
    lame_first,
    shear_mod,
    buoyancy,
    adj_out,
    kern_out,
    now,
    prev,
    mid,
    lame,
    shear,
    buoy,
    xlo,
    xhi,
    ylo,
    yhi,
    row_first,
    row_last,
    mod_send,
    mod_recv,
    low_stress,
    totals,
    share_send,
    share_recv,
    cells,
    amps,
    load_sem,
    send_sem,
    recv_sem,
):
    groups, count_x, count_y = sizes
    receivers, _, cells_x, cells_y, depth = adj_now.shape
    fields = receivers + 1
    grp = lax.axis_index("grp")
    gx = lax.axis_index("gx")
    gy = lax.axis_index("gy")
    has_down = gx > 0
    has_up = gx < count_x - 1
    has_left = gy > 0
    has_right = gy < count_y - 1
    corner_ul = jnp.logical_and(has_up, has_left)
    corner_dr = jnp.logical_and(has_down, has_right)
    down = (grp, gx - 1, gy)
    up = (grp, gx + 1, gy)
    left = (grp, gx, gy - 1)
    right = (grp, gx, gy + 1)
    up_left = (grp, gx + 1, gy - 1)
    down_right = (grp, gx - 1, gy + 1)
    peers = [(lax.rem(grp + d, groups), gx, gy) for d in range(1, groups)]
    sides = (
        (has_down, down),
        (has_up, up),
        (has_left, left),
        (has_right, right),
        (corner_ul, up_left),
        (corner_dr, down_right),
    )

    loads = [
        (adj_now, now.at[pl.ds(0, receivers)]),
        (fwd_now, now.at[receivers]),
        (lame_first, lame.at[pl.ds(1, cells_x)]),
        (shear_mod, shear.at[pl.ds(1, cells_x)]),
        (adj_prev, prev.at[pl.ds(0, receivers)]),
        (fwd_prev, prev.at[receivers]),
        (buoyancy, buoy),
    ]
    loads = [pltpu.make_async_copy(src, dst, load_sem.at[i]) for i, (src, dst) in enumerate(loads)]
    for copy in loads:
        copy.start()

    barrier = pltpu.get_barrier_semaphore()
    expected = jnp.int32(groups - 1)
    for there, where in sides:
        expected = expected + there.astype(jnp.int32)

        @pl.when(there)
        def _():
            pl.semaphore_signal(barrier, inc=1, device_id=where, device_id_type=MESH)

    for where in peers:
        pl.semaphore_signal(barrier, inc=1, device_id=where, device_id_type=MESH)

    for f in range(fields):
        master = f == receivers
        cells[f] = master_cell[0] if master else receiver_cell[f]
        lag = master_lag[0] if master else receiver_lag[f]
        for k in range(STEPS):
            for c in range(3):
                spot = (f * STEPS + k) * 3 + c
                amps[spot] = master_trace[c, lag + k] if master else receiver_trace[c, f, lag + k]

    @pl.when(jnp.logical_not(has_down))
    def _():
        xlo[...] = jnp.zeros_like(xlo)
        lame[0] = jnp.zeros_like(lame[0])
        shear[0] = jnp.zeros_like(shear[0])

    @pl.when(jnp.logical_not(has_up))
    def _():
        xhi[...] = jnp.zeros_like(xhi)

    @pl.when(jnp.logical_not(has_left))
    def _():
        ylo[:, :, 0:cells_x] = jnp.zeros_like(ylo[:, :, 0:cells_x])
        mod_recv[...] = jnp.zeros_like(mod_recv)

    @pl.when(jnp.logical_not(has_right))
    def _():
        yhi[:, :, 1 : cells_x + 1] = jnp.zeros_like(yhi[:, :, 1 : cells_x + 1])

    @pl.when(jnp.logical_not(corner_ul))
    def _():
        ylo[:, :, cells_x] = jnp.zeros_like(ylo[:, :, cells_x])

    @pl.when(jnp.logical_not(corner_dr))
    def _():
        yhi[:, :, 0] = jnp.zeros_like(yhi[:, :, 0])

    row_first[...] = jnp.zeros_like(row_first)
    row_last[...] = jnp.zeros_like(row_last)

    for copy in loads[:4]:
        copy.wait()

    def pack(f, carry):
        for c in range(3):
            for x in range(cells_x):
                row_first[0, c, x, pl.ds(f, 1), :] = now[f, c, x, 0:1, :]
                row_last[0, c, x, pl.ds(f, 1), :] = now[f, c, x, cells_y - 1 : cells_y, :]
        return carry

    lax.fori_loop(0, fields, pack, 0)
    for x in range(cells_x):
        mod_send[x : x + 1] = lame[x + 1, cells_y - 1 : cells_y, :]
        mod_send[cells_x + x : cells_x + x + 1] = shear[x + 1, cells_y - 1 : cells_y, :]

    pl.semaphore_wait(barrier, expected)

    number = [0]

    def remote(src, dst, where):
        i = number[0]
        number[0] += 1
        return pltpu.make_async_remote_copy(
            src_ref=src,
            dst_ref=dst,
            send_sem=send_sem.at[i],
            recv_sem=recv_sem.at[i],
            device_id=where,
            device_id_type=MESH,
        )

    def rows(k):
        return [
            (remote(row_first.at[k, :, cells_x - 1], yhi.at[k, :, 0], up_left), corner_ul, corner_dr),
            (remote(row_last.at[k, :, 0], ylo.at[k, :, cells_x], down_right), corner_dr, corner_ul),
            (remote(row_first.at[k], yhi.at[k, :, pl.ds(1, cells_x)], left), has_left, has_right),
            (remote(row_last.at[k], ylo.at[k, :, pl.ds(0, cells_x)], right), has_right, has_left),
        ]

    def start(copies):
        for copy, sends, _ in copies:
            pl.when(sends)(copy.start)

    def arrive(copies):
        for copy, _, gets in copies:
            pl.when(gets)(copy.wait_recv)

    def sent(copies):
        for copy, sends, _ in copies:
            pl.when(sends)(copy.wait_send)

    last = cells_x - 1
    group = pl.ds(0, receivers)
    first_round = [
        (remote(adj_now.at[:, :, 0], xhi.at[0, group], down), has_down, has_up),
        (remote(adj_now.at[:, :, last], xlo.at[0, group], up), has_up, has_down),
        (remote(fwd_now.at[:, 0], xhi.at[0, receivers], down), has_down, has_up),
        (remote(fwd_now.at[:, last], xlo.at[0, receivers], up), has_up, has_down),
        (remote(lame_first.at[last], lame.at[0], up), has_up, has_down),
        (remote(shear_mod.at[last], shear.at[0], up), has_up, has_down),
        (remote(mod_send, mod_recv, right), has_right, has_left),
    ] + rows(0)
    start(first_round)

    row_at = lax.broadcasted_iota(jnp.int32, (cells_y, depth), 0)
    lane_at = lax.broadcasted_iota(jnp.int32, (cells_y, depth), 1)
    flat_at = row_at * depth + lane_at
    top = row_at == 0
    bottom = row_at == cells_y - 1
    front = lane_at == 0
    back = lane_at == depth - 1
    plane_cells = cells_y * count_y * depth
    first_cell = gx * cells_x * plane_cells + gy * cells_y * depth

    def next_z(v):
        return jnp.where(back, 0.0, pltpu.roll(v, depth - 1, 1))

    def last_z(v):
        return jnp.where(front, 0.0, pltpu.roll(v, 1, 1))

    def next_y(v, row):
        return jnp.where(bottom, row, pltpu.roll(v, cells_y - 1, 0))

    def last_y(v, row):
        return jnp.where(top, row, pltpu.roll(v, 1, 0))

    def wall(k):
        for x in range(cells_x):
            here = [ylo[k, c, x] for c in range(3)]
            beside = [ylo[k, c, x + 1] for c in range(3)]
            above = [row_first[k, c, x] for c in range(3)]
            lam = mod_recv[x : x + 1]
            mu = mod_recv[cells_x + x : cells_x + x + 1]
            grad_y = [above[c] - here[c] for c in range(3)]
            xy = grad_y[0] + (beside[1] - here[1])
            yz = (next_z(here[1]) - here[1]) + grad_y[2]
            dilation = (beside[0] - here[0]) + grad_y[1] + (next_z(here[2]) - here[2])
            low_stress[k, 0, x] = mu * xy
            low_stress[k, 1, x] = lam * dilation + 2.0 * mu * grad_y[1]
            low_stress[k, 2, x] = mu * yz

    def step(k, f, state, earlier, put):
        one = pl.ds(f, 1)

        def row(c, x):
            return yhi[k, c, x + 1, one, :]

        here = [xlo[k, f, c] for c in range(3)]
        lam = lame[0]
        mu = shear[0]
        after = [state[f, c, 0] for c in range(3)]
        across = [next_y(here[c], row(c, -1)) for c in range(2)]
        along = [next_z(here[c]) for c in (0, 2)]
        xx = after[0] - here[0]
        dilation = xx + (across[1] - here[1]) + (along[1] - here[2])
        low = [
            lam * dilation + 2.0 * mu * xx,
            mu * ((across[0] - here[0]) + (after[1] - here[1])),
            mu * ((along[0] - here[0]) + (after[2] - here[2])),
        ]
        cell = cells[f]
        amp = [amps[(f * STEPS + k) * 3 + c] for c in range(3)]
        for x in range(cells_x):
            here = after
            after = [state[f, c, x + 1] if x < last else xhi[k, f, c] for c in range(3)]
            lam = lame[x + 1]
            mu = shear[x + 1]
            twice = 2.0 * mu
            gx_ = [after[c] - here[c] for c in range(3)]
            gy_ = [next_y(here[c], row(c, x)) - here[c] for c in range(3)]
            gz_ = [next_z(here[c]) - here[c] for c in range(3)]
            spread = lam * (gx_[0] + gy_[1] + gz_[2])
            xx = spread + twice * gx_[0]
            yy = spread + twice * gy_[1]
            zz = spread + twice * gz_[2]
            xy = mu * (gy_[0] + gx_[1])
            xz = mu * (gz_[0] + gx_[2])
            yz = mu * (gz_[1] + gy_[2])
            wall_xy, wall_yy, wall_yz = [low_stress[k, j, x, one, :] for j in range(3)]
            force = [
                (xx - low[0]) + (xy - last_y(xy, wall_xy)) + (xz - last_z(xz)),
                (xy - low[1]) + (yy - last_y(yy, wall_yy)) + (yz - last_z(yz)),
                (xz - low[2]) + (yz - last_y(yz, wall_yz)) + (zz - last_z(zz)),
            ]
            low = [xx, xy, xz]
            placed = flat_at == cell - (first_cell + x * plane_cells)
            scaled = time_step_sq * buoy[x]
            for c in range(3):
                moved = force[c] + jnp.where(placed, amp[c], 0.0)
                put(f, c, x, 2.0 * here[c] - earlier[f, c, x] + scaled * moved)

    def strain(planes, rows):
        for x in range(cells_x):
            here, after = planes[x], planes[x + 1]
            gx_ = [after[c] - here[c] for c in range(3)]
            gy_ = [next_y(here[c], rows[x][c]) - here[c] for c in range(3)]
            gz_ = [next_z(here[c]) - here[c] for c in range(3)]
            yield (
                gx_[0],
                gy_[1],
                gz_[2],
                gy_[0] + gx_[1],
                gz_[0] + gx_[2],
                gz_[1] + gy_[2],
            )

    def correlate(k, state):
        def summed(load):
            total = load(0)
            for f in range(1, receivers):
                total = total + load(f)
            return total

        whole, master = [], []
        for x in range(cells_x + 1):
            if x < cells_x:
                whole.append([summed(lambda f: state[f, c, x]) for c in range(3)])
                master.append([state[receivers, c, x] for c in range(3)])
            else:
                whole.append([summed(lambda f: xhi[k, f, c]) for c in range(3)])
                master.append([xhi[k, receivers, c] for c in range(3)])
        whole_rows = [
            [summed(lambda f: yhi[k, c, x + 1, f : f + 1, :]) for c in range(3)]
            for x in range(cells_x)
        ]
        master_rows = [
            [yhi[k, c, x + 1, receivers : receivers + 1, :] for c in range(3)]
            for x in range(cells_x)
        ]
        pairs = zip(strain(whole, whole_rows), strain(master, master_rows))
        for x, (a, b) in enumerate(pairs):
            swell = (a[0] + a[1] + a[2]) * (b[0] + b[1] + b[2])
            twist = 2.0 * (a[0] * b[0] + a[1] * b[1] + a[2] * b[2])
            twist = twist + (a[3] * b[3] + a[4] * b[4] + a[5] * b[5])
            if k == 0:
                totals[0, x] = swell
                totals[1, x] = twist
            else:
                totals[0, x] += swell
                totals[1, x] += twist

    for copy in loads[4:]:
        copy.wait()
    arrive(first_round)

    def put_mid(f, c, x, value):
        mid[f, c, x] = value
        row_first[1, c, x, pl.ds(f, 1), :] = value[0:1]
        row_last[1, c, x, pl.ds(f, 1), :] = value[cells_y - 1 : cells_y]

    def first_step(f, carry):
        step(0, f, now, prev, put_mid)
        return carry

    wall(0)
    lax.fori_loop(0, fields, first_step, 0)

    second_round = [
        (remote(mid.at[:, :, 0], xhi.at[1], down), has_down, has_up),
        (remote(mid.at[:, :, last], xlo.at[1], up), has_up, has_down),
    ] + rows(1)
    start(second_round)
    correlate(0, now)
    arrive(second_round)
    correlate(1, mid)

    share = depth // groups
    lane_part = lane_at // share
    for g in range(groups):
        for j in range(2):
            packed = None
            for x in range(cells_x):
                turn = (share * (x - g)) % depth
                piece = totals[j, x] if turn == 0 else pltpu.roll(totals[j, x], turn, 1)
                packed = piece if packed is None else jnp.where(lane_part == x, piece, packed)
            share_send[g, j] = packed
    third_round = [
        (remote(share_send.at[peers[d][0]], share_recv.at[d], peers[d]), True, True)
        for d in range(groups - 1)
    ]
    for copy, _, _ in third_round:
        copy.start()

    def put_out(f, c, x, value):
        adj_out[f, c, x] = value

    def last_step(f, carry):
        step(1, f, mid, now, put_out)
        return carry

    wall(1)
    lax.fori_loop(0, receivers, last_step, 0)

    for copy, _, _ in third_round:
        copy.wait_recv()
    scale_out = 1.0 / (STEPS * receivers * groups)
    for j in range(2):
        part = share_send[grp, j]
        for d in range(groups - 1):
            part = part + share_recv[d, j]
        part = part * scale_out
        for x in range(cells_x):
            piece = part if x == 0 else pltpu.roll(part, depth - share * x, 1)
            kern_out[j, x] = piece[:, 0:share]
    sent(first_round)
    sent(second_round)
    for copy, _, _ in third_round:
        copy.wait_send()


def local(
    fwd_now,
    fwd_prev,
    adj_now,
    adj_prev,
    lame_first,
    shear_mod,
    buoyancy,
    master_cell,
    master_lag,
    master_trace,
    receiver_cell,
    receiver_lag,
    receiver_trace,
):
    cells_x, cells_y, depth = lame_first.shape
    receivers = adj_now.shape[0]
    fields = receivers + 1
    sizes = tuple(lax.axis_size(axis) for axis in ("grp", "gx", "gy"))
    groups = sizes[0]
    lanes = -(-fields // 8) * 8
    block = (fields, 3, cells_x, cells_y, depth)
    scalars = pl.BlockSpec(memory_space=pltpu.SMEM)
    whole = pl.BlockSpec(memory_space=pl.ANY)
    vector = pl.BlockSpec(memory_space=pltpu.VMEM)

    def room(*shape):
        return pltpu.VMEM(shape, jnp.float32)

    return pl.pallas_call(
        functools.partial(kernel, sizes),
        out_shape=(
            jax.ShapeDtypeStruct(adj_now.shape, jnp.float32),
            jax.ShapeDtypeStruct((2, cells_x, cells_y, depth // groups), jnp.float32),
        ),
        in_specs=[scalars] * 6 + [whole] * 7,
        out_specs=(vector, vector),
        scratch_shapes=[
            room(*block),
            room(*block),
            room(*block),
            room(cells_x + 1, cells_y, depth),
            room(cells_x + 1, cells_y, depth),
            room(cells_x, cells_y, depth),
            room(STEPS, fields, 3, cells_y, depth),
            room(STEPS, fields, 3, cells_y, depth),
            room(STEPS, 3, cells_x + 1, lanes, depth),
            room(STEPS, 3, cells_x + 1, lanes, depth),
            room(STEPS, 3, cells_x, lanes, depth),
            room(STEPS, 3, cells_x, lanes, depth),
            room(2 * cells_x, depth),
            room(2 * cells_x, depth),
            room(STEPS, 3, cells_x, lanes, depth),
            room(2, cells_x, cells_y, depth),
            room(groups, 2, cells_y, depth),
            room(groups - 1, 2, cells_y, depth),
            pltpu.SMEM((fields,), jnp.int32),
            pltpu.SMEM((fields * STEPS * 3,), jnp.float32),
            pltpu.SemaphoreType.DMA((7,)),
            pltpu.SemaphoreType.DMA((32,)),
            pltpu.SemaphoreType.DMA((32,)),
        ],
        compiler_params=pltpu.CompilerParams(
            collective_id=0, has_side_effects=True, vmem_limit_bytes=56 * 1024 * 1024
        ),
    )(
        master_cell,
        master_lag,
        master_trace.T,
        receiver_cell,
        receiver_lag,
        receiver_trace.transpose(2, 0, 1),
        fwd_now,
        fwd_prev,
        adj_now,
        adj_prev,
        lame_first,
        shear_mod,
        buoyancy,
    )


def solution(mesh):
    in_specs = (
        P(None, "gx", "gy", None),
        P(None, "gx", "gy", None),
        P("grp", None, "gx", "gy", None),
        P("grp", None, "gx", "gy", None),
        P("gx", "gy", None),
        P("gx", "gy", None),
        P("gx", "gy", None),
        P(),
        P(),
        P(),
        P("grp"),
        P("grp"),
        P("grp", None, None),
    )
    out_specs = (P("grp", None, "gx", "gy", None), P(None, "gx", "gy", "grp"))
    return jax.shard_map(local, mesh=mesh, in_specs=in_specs, out_specs=out_specs, check_vma=False)
```

```python
import functools

import jax
import jax.numpy as jnp
from jax import lax
from jax.experimental import pallas as pl
from jax.experimental.pallas import tpu as pltpu
from jax.sharding import PartitionSpec as P

STEPS = 2
MESH = pl.DeviceIdType.MESH

time_step_sq = 0.0625


def kernel(
    sizes,
    master_cell,
    master_lag,
    master_trace,
    receiver_cell,
    receiver_lag,
    receiver_trace,
    fwd_now,
    fwd_prev,
    adj_now,
    adj_prev,
    lame_first,
    shear_mod,
    buoyancy,
    adj_out,
    kern_out,
    now,
    prev,
    mid,
    lame,
    shear,
    buoy,
    xlo,
    xhi,
    ylo,
    yhi,
    row_first,
    row_last,
    mod_send,
    mod_recv,
    low_stress,
    totals,
    share_send,
    share_recv,
    cells,
    amps,
    master_trace_s,
    receiver_cell_s,
    receiver_lag_s,
    receiver_trace_s,
    load_sem,
    send_sem,
    recv_sem,
):
    groups, count_x, count_y = sizes
    receivers, _, cells_x, cells_y, depth = adj_now.shape
    fields = receivers + 1
    grp = lax.axis_index("grp")
    gx = lax.axis_index("gx")
    gy = lax.axis_index("gy")
    has_down = gx > 0
    has_up = gx < count_x - 1
    has_left = gy > 0
    has_right = gy < count_y - 1
    corner_ul = jnp.logical_and(has_up, has_left)
    corner_dr = jnp.logical_and(has_down, has_right)
    down = (grp, gx - 1, gy)
    up = (grp, gx + 1, gy)
    left = (grp, gx, gy - 1)
    right = (grp, gx, gy + 1)
    up_left = (grp, gx + 1, gy - 1)
    down_right = (grp, gx - 1, gy + 1)
    peers = [(lax.rem(grp + d, groups), gx, gy) for d in range(1, groups)]
    sides = (
        (has_down, down),
        (has_up, up),
        (has_left, left),
        (has_right, right),
        (corner_ul, up_left),
        (corner_dr, down_right),
    )

    loads = [
        (adj_now, now.at[pl.ds(0, receivers)]),
        (fwd_now, now.at[receivers]),
        (lame_first, lame.at[pl.ds(1, cells_x)]),
        (shear_mod, shear.at[pl.ds(1, cells_x)]),
        (adj_prev, prev.at[pl.ds(0, receivers)]),
        (fwd_prev, prev.at[receivers]),
        (buoyancy, buoy),
        (master_trace, master_trace_s),
        (receiver_cell, receiver_cell_s),
        (receiver_lag, receiver_lag_s),
        (receiver_trace, receiver_trace_s),
    ]
    loads = [pltpu.make_async_copy(src, dst, load_sem.at[i]) for i, (src, dst) in enumerate(loads)]
    for copy in loads:
        copy.start()

    barrier = pltpu.get_barrier_semaphore()
    expected = jnp.int32(groups - 1)
    for there, where in sides:
        expected = expected + there.astype(jnp.int32)

        @pl.when(there)
        def _():
            pl.semaphore_signal(barrier, inc=1, device_id=where, device_id_type=MESH)

    for where in peers:
        pl.semaphore_signal(barrier, inc=1, device_id=where, device_id_type=MESH)

    @pl.when(jnp.logical_not(has_down))
    def _():
        xlo[...] = jnp.zeros_like(xlo)
        lame[0] = jnp.zeros_like(lame[0])
        shear[0] = jnp.zeros_like(shear[0])

    @pl.when(jnp.logical_not(has_up))
    def _():
        xhi[...] = jnp.zeros_like(xhi)

    @pl.when(jnp.logical_not(has_left))
    def _():
        ylo[:, :, 0:cells_x] = jnp.zeros_like(ylo[:, :, 0:cells_x])
        mod_recv[...] = jnp.zeros_like(mod_recv)

    @pl.when(jnp.logical_not(has_right))
    def _():
        yhi[:, :, 1 : cells_x + 1] = jnp.zeros_like(yhi[:, :, 1 : cells_x + 1])

    @pl.when(jnp.logical_not(corner_ul))
    def _():
        ylo[:, :, cells_x] = jnp.zeros_like(ylo[:, :, cells_x])

    @pl.when(jnp.logical_not(corner_dr))
    def _():
        yhi[:, :, 0] = jnp.zeros_like(yhi[:, :, 0])

    row_first[...] = jnp.zeros_like(row_first)
    row_last[...] = jnp.zeros_like(row_last)

    for copy in loads[:4]:
        copy.wait()

    def pack(f, carry):
        for c in range(3):
            for x in range(cells_x):
                row_first[0, c, x, pl.ds(f, 1), :] = now[f, c, x, 0:1, :]
                row_last[0, c, x, pl.ds(f, 1), :] = now[f, c, x, cells_y - 1 : cells_y, :]
        return carry

    lax.fori_loop(0, fields, pack, 0)
    for x in range(cells_x):
        mod_send[x : x + 1] = lame[x + 1, cells_y - 1 : cells_y, :]
        mod_send[cells_x + x : cells_x + x + 1] = shear[x + 1, cells_y - 1 : cells_y, :]

    pl.semaphore_wait(barrier, expected)

    number = [0]

    def remote(src, dst, where):
        i = number[0]
        number[0] += 1
        return pltpu.make_async_remote_copy(
            src_ref=src,
            dst_ref=dst,
            send_sem=send_sem.at[i],
            recv_sem=recv_sem.at[i],
            device_id=where,
            device_id_type=MESH,
        )

    def rows(k):
        return [
            (remote(row_first.at[k, :, cells_x - 1], yhi.at[k, :, 0], up_left), corner_ul, corner_dr),
            (remote(row_last.at[k, :, 0], ylo.at[k, :, cells_x], down_right), corner_dr, corner_ul),
            (remote(row_first.at[k], yhi.at[k, :, pl.ds(1, cells_x)], left), has_left, has_right),
            (remote(row_last.at[k], ylo.at[k, :, pl.ds(0, cells_x)], right), has_right, has_left),
        ]

    def start(copies):
        for copy, sends, _ in copies:
            pl.when(sends)(copy.start)

    def arrive(copies):
        for copy, _, gets in copies:
            pl.when(gets)(copy.wait_recv)

    def sent(copies):
        for copy, sends, _ in copies:
            pl.when(sends)(copy.wait_send)

    last = cells_x - 1
    group = pl.ds(0, receivers)
    first_round = [
        (remote(adj_now.at[:, :, 0], xhi.at[0, group], down), has_down, has_up),
        (remote(adj_now.at[:, :, last], xlo.at[0, group], up), has_up, has_down),
        (remote(fwd_now.at[:, 0], xhi.at[0, receivers], down), has_down, has_up),
        (remote(fwd_now.at[:, last], xlo.at[0, receivers], up), has_up, has_down),
        (remote(lame_first.at[last], lame.at[0], up), has_up, has_down),
        (remote(shear_mod.at[last], shear.at[0], up), has_up, has_down),
        (remote(mod_send, mod_recv, right), has_right, has_left),
    ] + rows(0)
    start(first_round)

    for copy in loads[4:]:
        copy.wait()

    for f in range(fields):
        master = f == receivers
        cells[f] = master_cell[0] if master else receiver_cell_s[f]
        lag = master_lag[0] if master else receiver_lag_s[f]
        for k in range(STEPS):
            for c in range(3):
                spot = (f * STEPS + k) * 3 + c
                amps[spot] = master_trace_s[c, lag + k] if master else receiver_trace_s[c, f, lag + k]

    row_at = lax.broadcasted_iota(jnp.int32, (cells_y, depth), 0)
    lane_at = lax.broadcasted_iota(jnp.int32, (cells_y, depth), 1)
    flat_at = row_at * depth + lane_at
    top = row_at == 0
    bottom = row_at == cells_y - 1
    front = lane_at == 0
    back = lane_at == depth - 1
    plane_cells = cells_y * count_y * depth
    first_cell = gx * cells_x * plane_cells + gy * cells_y * depth

    def next_z(v):
        return jnp.where(back, 0.0, pltpu.roll(v, depth - 1, 1))

    def last_z(v):
        return jnp.where(front, 0.0, pltpu.roll(v, 1, 1))

    def next_y(v, row):
        return jnp.where(bottom, row, pltpu.roll(v, cells_y - 1, 0))

    def last_y(v, row):
        return jnp.where(top, row, pltpu.roll(v, 1, 0))

    def wall(k):
        for x in range(cells_x):
            here = [ylo[k, c, x] for c in range(3)]
            beside = [ylo[k, c, x + 1] for c in range(3)]
            above = [row_first[k, c, x] for c in range(3)]
            lam = mod_recv[x : x + 1]
            mu = mod_recv[cells_x + x : cells_x + x + 1]
            grad_y = [above[c] - here[c] for c in range(3)]
            xy = grad_y[0] + (beside[1] - here[1])
            yz = (next_z(here[1]) - here[1]) + grad_y[2]
            dilation = (beside[0] - here[0]) + grad_y[1] + (next_z(here[2]) - here[2])
            low_stress[k, 0, x] = mu * xy
            low_stress[k, 1, x] = lam * dilation + 2.0 * mu * grad_y[1]
            low_stress[k, 2, x] = mu * yz

    def step(k, f, state, earlier, put):
        one = pl.ds(f, 1)

        def row(c, x):
            return yhi[k, c, x + 1, one, :]

        here = [xlo[k, f, c] for c in range(3)]
        lam = lame[0]
        mu = shear[0]
        after = [state[f, c, 0] for c in range(3)]
        across = [next_y(here[c], row(c, -1)) for c in range(2)]
        along = [next_z(here[c]) for c in (0, 2)]
        xx = after[0] - here[0]
        dilation = xx + (across[1] - here[1]) + (along[1] - here[2])
        low = [
            lam * dilation + 2.0 * mu * xx,
            mu * ((across[0] - here[0]) + (after[1] - here[1])),
            mu * ((along[0] - here[0]) + (after[2] - here[2])),
        ]
        cell = cells[f]
        amp = [amps[(f * STEPS + k) * 3 + c] for c in range(3)]
        for x in range(cells_x):
            here = after
            after = [state[f, c, x + 1] if x < last else xhi[k, f, c] for c in range(3)]
            lam = lame[x + 1]
            mu = shear[x + 1]
            twice = 2.0 * mu
            gx_ = [after[c] - here[c] for c in range(3)]
            gy_ = [next_y(here[c], row(c, x)) - here[c] for c in range(3)]
            gz_ = [next_z(here[c]) - here[c] for c in range(3)]
            spread = lam * (gx_[0] + gy_[1] + gz_[2])
            xx = spread + twice * gx_[0]
            yy = spread + twice * gy_[1]
            zz = spread + twice * gz_[2]
            xy = mu * (gy_[0] + gx_[1])
            xz = mu * (gz_[0] + gx_[2])
            yz = mu * (gz_[1] + gy_[2])
            wall_xy, wall_yy, wall_yz = [low_stress[k, j, x, one, :] for j in range(3)]
            force = [
                (xx - low[0]) + (xy - last_y(xy, wall_xy)) + (xz - last_z(xz)),
                (xy - low[1]) + (yy - last_y(yy, wall_yy)) + (yz - last_z(yz)),
                (xz - low[2]) + (yz - last_y(yz, wall_yz)) + (zz - last_z(zz)),
            ]
            low = [xx, xy, xz]
            placed = flat_at == cell - (first_cell + x * plane_cells)
            scaled = time_step_sq * buoy[x]
            for c in range(3):
                moved = force[c] + jnp.where(placed, amp[c], 0.0)
                put(f, c, x, 2.0 * here[c] - earlier[f, c, x] + scaled * moved)

    def strain(planes, rows):
        for x in range(cells_x):
            here, after = planes[x], planes[x + 1]
            gx_ = [after[c] - here[c] for c in range(3)]
            gy_ = [next_y(here[c], rows[x][c]) - here[c] for c in range(3)]
            gz_ = [next_z(here[c]) - here[c] for c in range(3)]
            yield (
                gx_[0],
                gy_[1],
                gz_[2],
                gy_[0] + gx_[1],
                gz_[0] + gx_[2],
                gz_[1] + gy_[2],
            )

    def correlate(k, state):
        def summed(load):
            total = load(0)
            for f in range(1, receivers):
                total = total + load(f)
            return total

        whole, master = [], []
        for x in range(cells_x + 1):
            if x < cells_x:
                whole.append([summed(lambda f: state[f, c, x]) for c in range(3)])
                master.append([state[receivers, c, x] for c in range(3)])
            else:
                whole.append([summed(lambda f: xhi[k, f, c]) for c in range(3)])
                master.append([xhi[k, receivers, c] for c in range(3)])
        whole_rows = [
            [summed(lambda f: yhi[k, c, x + 1, f : f + 1, :]) for c in range(3)]
            for x in range(cells_x)
        ]
        master_rows = [
            [yhi[k, c, x + 1, receivers : receivers + 1, :] for c in range(3)]
            for x in range(cells_x)
        ]
        pairs = zip(strain(whole, whole_rows), strain(master, master_rows))
        for x, (a, b) in enumerate(pairs):
            swell = (a[0] + a[1] + a[2]) * (b[0] + b[1] + b[2])
            twist = 2.0 * (a[0] * b[0] + a[1] * b[1] + a[2] * b[2])
            twist = twist + (a[3] * b[3] + a[4] * b[4] + a[5] * b[5])
            if k == 0:
                totals[0, x] = swell
                totals[1, x] = twist
            else:
                totals[0, x] += swell
                totals[1, x] += twist

    arrive(first_round)

    def put_mid(f, c, x, value):
        mid[f, c, x] = value
        row_first[1, c, x, pl.ds(f, 1), :] = value[0:1]
        row_last[1, c, x, pl.ds(f, 1), :] = value[cells_y - 1 : cells_y]

    def first_step(f, carry):
        step(0, f, now, prev, put_mid)
        return carry

    wall(0)
    lax.fori_loop(0, fields, first_step, 0)

    second_round = [
        (remote(mid.at[:, :, 0], xhi.at[1], down), has_down, has_up),
        (remote(mid.at[:, :, last], xlo.at[1], up), has_up, has_down),
    ] + rows(1)
    start(second_round)
    correlate(0, now)
    arrive(second_round)
    correlate(1, mid)

    share = depth // groups
    lane_part = lane_at // share
    for g in range(groups):
        for j in range(2):
            packed = None
            for x in range(cells_x):
                turn = (share * (x - g)) % depth
                piece = totals[j, x] if turn == 0 else pltpu.roll(totals[j, x], turn, 1)
                packed = piece if packed is None else jnp.where(lane_part == x, piece, packed)
            share_send[g, j] = packed
    third_round = [
        (remote(share_send.at[peers[d][0]], share_recv.at[d], peers[d]), True, True)
        for d in range(groups - 1)
    ]
    for copy, _, _ in third_round:
        copy.start()

    def put_out(f, c, x, value):
        adj_out[f, c, x] = value

    def last_step(f, carry):
        step(1, f, mid, now, put_out)
        return carry

    wall(1)
    lax.fori_loop(0, receivers, last_step, 0)

    for copy, _, _ in third_round:
        copy.wait_recv()
    scale_out = 1.0 / (STEPS * receivers * groups)
    for j in range(2):
        part = share_send[grp, j]
        for d in range(groups - 1):
            part = part + share_recv[d, j]
        part = part * scale_out
        for x in range(cells_x):
            piece = part if x == 0 else pltpu.roll(part, depth - share * x, 1)
            kern_out[j, x] = piece[:, 0:share]
    sent(first_round)
    sent(second_round)
    for copy, _, _ in third_round:
        copy.wait_send()


def local(
    fwd_now,
    fwd_prev,
    adj_now,
    adj_prev,
    lame_first,
    shear_mod,
    buoyancy,
    master_cell,
    master_lag,
    master_trace,
    receiver_cell,
    receiver_lag,
    receiver_trace,
):
    cells_x, cells_y, depth = lame_first.shape
    receivers = adj_now.shape[0]
    fields = receivers + 1
    sizes = tuple(lax.axis_size(axis) for axis in ("grp", "gx", "gy"))
    groups = sizes[0]
    lanes = -(-fields // 8) * 8
    block = (fields, 3, cells_x, cells_y, depth)
    scalar = pl.BlockSpec(memory_space=pltpu.SMEM)
    whole = pl.BlockSpec(memory_space=pltpu.HBM)
    vector = pl.BlockSpec(memory_space=pltpu.VMEM)

    def room(*shape):
        return pltpu.VMEM(shape, jnp.float32)

    def stay(value):
        return pltpu.with_memory_space_constraint(value, pltpu.HBM)

    return pl.pallas_call(
        functools.partial(kernel, sizes),
        out_shape=(
            pltpu.VMEM(adj_now.shape, jnp.float32),
            pltpu.VMEM((2, cells_x, cells_y, depth // groups), jnp.float32),
        ),
        in_specs=[scalar] * 2 + [whole] * 11,
        out_specs=(vector, vector),
        scratch_shapes=[
            room(*block),
            room(*block),
            room(*block),
            room(cells_x + 1, cells_y, depth),
            room(cells_x + 1, cells_y, depth),
            room(cells_x, cells_y, depth),
            room(STEPS, fields, 3, cells_y, depth),
            room(STEPS, fields, 3, cells_y, depth),
            room(STEPS, 3, cells_x + 1, lanes, depth),
            room(STEPS, 3, cells_x + 1, lanes, depth),
            room(STEPS, 3, cells_x, lanes, depth),
            room(STEPS, 3, cells_x, lanes, depth),
            room(2 * cells_x, depth),
            room(2 * cells_x, depth),
            room(STEPS, 3, cells_x, lanes, depth),
            room(2, cells_x, cells_y, depth),
            room(groups, 2, cells_y, depth),
            room(groups - 1, 2, cells_y, depth),
            pltpu.SMEM((fields,), jnp.int32),
            pltpu.SMEM((fields * STEPS * 3,), jnp.float32),
            pltpu.SMEM((3,) + master_trace.shape[:1], jnp.float32),
            pltpu.SMEM((receivers,), jnp.int32),
            pltpu.SMEM((receivers,), jnp.int32),
            pltpu.SMEM((3,) + receiver_trace.shape[:2], jnp.float32),
            pltpu.SemaphoreType.DMA((11,)),
            pltpu.SemaphoreType.DMA((32,)),
            pltpu.SemaphoreType.DMA((32,)),
        ],
        compiler_params=pltpu.CompilerParams(
            collective_id=0, has_side_effects=True, vmem_limit_bytes=32 * 1024 * 1024
        ),
    )(
        master_cell,
        master_lag,
        stay(master_trace.T),
        stay(receiver_cell),
        stay(receiver_lag),
        stay(receiver_trace.transpose(2, 0, 1)),
        stay(fwd_now),
        stay(fwd_prev),
        stay(adj_now),
        stay(adj_prev),
        stay(lame_first),
        stay(shear_mod),
        stay(buoyancy),
    )


def solution(mesh):
    in_specs = (
        P(None, "gx", "gy", None),
        P(None, "gx", "gy", None),
        P("grp", None, "gx", "gy", None),
        P("grp", None, "gx", "gy", None),
        P("gx", "gy", None),
        P("gx", "gy", None),
        P("gx", "gy", None),
        P(),
        P(),
        P(),
        P("grp"),
        P("grp"),
        P("grp", None, None),
    )
    out_specs = (P("grp", None, "gx", "gy", None), P(None, "gx", "gy", "grp"))
    return jax.shard_map(local, mesh=mesh, in_specs=in_specs, out_specs=out_specs, check_vma=False)
```

```python
import functools

import jax
import jax.numpy as jnp
from jax import lax
from jax.experimental import pallas as pl
from jax.experimental.pallas import tpu as pltpu
from jax.sharding import PartitionSpec as P

STEPS = 2
MESH = pl.DeviceIdType.MESH

time_step_sq = 0.0625


def kernel(
    sizes,
    master_cell,
    master_lag,
    master_trace,
    receiver_cell,
    receiver_lag,
    receiver_trace,
    fwd_now,
    fwd_prev,
    adj_now,
    adj_prev,
    lame_first,
    shear_mod,
    buoyancy,
    adj_out,
    kern_out,
    now,
    prev,
    mid,
    lame,
    shear,
    buoy,
    xlo,
    xhi,
    ylo,
    yhi,
    row_first,
    row_last,
    mod_send,
    mod_recv,
    low_stress,
    totals,
    share_send,
    share_recv,
    cells,
    amps,
    master_trace_s,
    receiver_cell_s,
    receiver_lag_s,
    receiver_trace_s,
    load_sem,
    send_sem,
    recv_sem,
):
    groups, count_x, count_y = sizes
    receivers, _, cells_x, cells_y, depth = adj_now.shape
    fields = receivers + 1
    grp = lax.axis_index("grp")
    gx = lax.axis_index("gx")
    gy = lax.axis_index("gy")
    has_down = gx > 0
    has_up = gx < count_x - 1
    has_left = gy > 0
    has_right = gy < count_y - 1
    corner_ul = jnp.logical_and(has_up, has_left)
    corner_dr = jnp.logical_and(has_down, has_right)
    down = (grp, gx - 1, gy)
    up = (grp, gx + 1, gy)
    left = (grp, gx, gy - 1)
    right = (grp, gx, gy + 1)
    up_left = (grp, gx + 1, gy - 1)
    down_right = (grp, gx - 1, gy + 1)
    peers = [(lax.rem(grp + d, groups), gx, gy) for d in range(1, groups)]
    sides = (
        (has_down, down),
        (has_up, up),
        (has_left, left),
        (has_right, right),
        (corner_ul, up_left),
        (corner_dr, down_right),
    )

    loads = [
        (adj_now, now.at[pl.ds(0, receivers)]),
        (fwd_now, now.at[receivers]),
        (lame_first, lame.at[pl.ds(1, cells_x)]),
        (shear_mod, shear.at[pl.ds(1, cells_x)]),
        (adj_prev, prev.at[pl.ds(0, receivers)]),
        (fwd_prev, prev.at[receivers]),
        (buoyancy, buoy),
        (master_trace, master_trace_s),
        (receiver_cell, receiver_cell_s),
        (receiver_lag, receiver_lag_s),
        (receiver_trace, receiver_trace_s),
    ]
    loads = [pltpu.make_async_copy(src, dst, load_sem.at[i]) for i, (src, dst) in enumerate(loads)]
    for copy in loads:
        copy.start()

    barrier = pltpu.get_barrier_semaphore()
    expected = jnp.int32(groups - 1)
    for there, where in sides:
        expected = expected + there.astype(jnp.int32)

        @pl.when(there)
        def _():
            pl.semaphore_signal(barrier, inc=1, device_id=where, device_id_type=MESH)

    for where in peers:
        pl.semaphore_signal(barrier, inc=1, device_id=where, device_id_type=MESH)

    @pl.when(jnp.logical_not(has_down))
    def _():
        xlo[...] = jnp.zeros_like(xlo)
        lame[0] = jnp.zeros_like(lame[0])
        shear[0] = jnp.zeros_like(shear[0])

    @pl.when(jnp.logical_not(has_up))
    def _():
        xhi[...] = jnp.zeros_like(xhi)

    @pl.when(jnp.logical_not(has_left))
    def _():
        ylo[:, :, 0:cells_x] = jnp.zeros_like(ylo[:, :, 0:cells_x])
        mod_recv[...] = jnp.zeros_like(mod_recv)

    @pl.when(jnp.logical_not(has_right))
    def _():
        yhi[:, :, 1 : cells_x + 1] = jnp.zeros_like(yhi[:, :, 1 : cells_x + 1])

    @pl.when(jnp.logical_not(corner_ul))
    def _():
        ylo[:, :, cells_x] = jnp.zeros_like(ylo[:, :, cells_x])

    @pl.when(jnp.logical_not(corner_dr))
    def _():
        yhi[:, :, 0] = jnp.zeros_like(yhi[:, :, 0])

    row_first[...] = jnp.zeros_like(row_first)
    row_last[...] = jnp.zeros_like(row_last)

    pl.semaphore_wait(barrier, expected)

    number = [0]

    def remote(src, dst, where):
        i = number[0]
        number[0] += 1
        return pltpu.make_async_remote_copy(
            src_ref=src,
            dst_ref=dst,
            send_sem=send_sem.at[i],
            recv_sem=recv_sem.at[i],
            device_id=where,
            device_id_type=MESH,
        )

    def rows(k):
        return [
            (remote(row_first.at[k, :, cells_x - 1], yhi.at[k, :, 0], up_left), corner_ul, corner_dr),
            (remote(row_last.at[k, :, 0], ylo.at[k, :, cells_x], down_right), corner_dr, corner_ul),
            (remote(row_first.at[k], yhi.at[k, :, pl.ds(1, cells_x)], left), has_left, has_right),
            (remote(row_last.at[k], ylo.at[k, :, pl.ds(0, cells_x)], right), has_right, has_left),
        ]

    def start(copies):
        for copy, sends, _ in copies:
            pl.when(sends)(copy.start)

    def arrive(copies):
        for copy, _, gets in copies:
            pl.when(gets)(copy.wait_recv)

    def sent(copies):
        for copy, sends, _ in copies:
            pl.when(sends)(copy.wait_send)

    last = cells_x - 1
    split = (receivers + 2) // 2
    group = pl.ds(0, split)
    rest = pl.ds(split, receivers - split)
    rest_all = pl.ds(split, fields - split)
    first_x = [
        (remote(adj_now.at[group, :, 0], xhi.at[0, group], down), has_down, has_up),
        (remote(adj_now.at[group, :, last], xlo.at[0, group], up), has_up, has_down),
    ]
    first_moduli = [
        (remote(lame_first.at[last], lame.at[0], up), has_up, has_down),
        (remote(shear_mod.at[last], shear.at[0], up), has_up, has_down),
        (remote(mod_send, mod_recv, right), has_right, has_left),
    ]
    first_rest = [
        (remote(adj_now.at[rest, :, 0], xhi.at[0, rest], down), has_down, has_up),
        (remote(adj_now.at[rest, :, last], xlo.at[0, rest], up), has_up, has_down),
        (remote(fwd_now.at[:, 0], xhi.at[0, receivers], down), has_down, has_up),
        (remote(fwd_now.at[:, last], xlo.at[0, receivers], up), has_up, has_down),
    ]
    first_rows = rows(0)
    start(first_moduli[:2])
    start(first_x)
    start(first_rest)

    for copy in loads[:4]:
        copy.wait()

    for f in range(fields):
        for c in range(3):
            for x in range(cells_x):
                row_first[0, c, x, f : f + 1, :] = now[f, c, x, 0:1, :]
                row_last[0, c, x, f : f + 1, :] = now[f, c, x, cells_y - 1 : cells_y, :]
    for x in range(cells_x):
        mod_send[x : x + 1] = lame[x + 1, cells_y - 1 : cells_y, :]
        mod_send[cells_x + x : cells_x + x + 1] = shear[x + 1, cells_y - 1 : cells_y, :]

    start(first_rows)
    start(first_moduli[2:])

    for copy in loads[4:]:
        copy.wait()

    for f in range(fields):
        master = f == receivers
        cells[f] = master_cell[0] if master else receiver_cell_s[f]
        lag = master_lag[0] if master else receiver_lag_s[f]
        for k in range(STEPS):
            for c in range(3):
                spot = (f * STEPS + k) * 3 + c
                amps[spot] = master_trace_s[c, lag + k] if master else receiver_trace_s[c, f, lag + k]

    row_at = lax.broadcasted_iota(jnp.int32, (cells_y, depth), 0)
    lane_at = lax.broadcasted_iota(jnp.int32, (cells_y, depth), 1)
    flat_at = row_at * depth + lane_at
    top = row_at == 0
    bottom = row_at == cells_y - 1
    front = lane_at == 0
    back = lane_at == depth - 1
    plane_cells = cells_y * count_y * depth
    first_cell = gx * cells_x * plane_cells + gy * cells_y * depth

    def next_z(v):
        return jnp.where(back, 0.0, pltpu.roll(v, depth - 1, 1))

    def last_z(v):
        return jnp.where(front, 0.0, pltpu.roll(v, 1, 1))

    def next_y(v, row):
        return jnp.where(bottom, row, pltpu.roll(v, cells_y - 1, 0))

    def last_y(v, row):
        return jnp.where(top, row, pltpu.roll(v, 1, 0))

    def wall(k):
        for x in range(cells_x):
            here = [ylo[k, c, x] for c in range(3)]
            beside = [ylo[k, c, x + 1] for c in range(3)]
            above = [row_first[k, c, x] for c in range(3)]
            lam = mod_recv[x : x + 1]
            mu = mod_recv[cells_x + x : cells_x + x + 1]
            grad_y = [above[c] - here[c] for c in range(3)]
            xy = grad_y[0] + (beside[1] - here[1])
            yz = (next_z(here[1]) - here[1]) + grad_y[2]
            dilation = (beside[0] - here[0]) + grad_y[1] + (next_z(here[2]) - here[2])
            low_stress[k, 0, x] = mu * xy
            low_stress[k, 1, x] = lam * dilation + 2.0 * mu * grad_y[1]
            low_stress[k, 2, x] = mu * yz

    def step(k, f, state, earlier, put):
        one = slice(f, f + 1)

        def row(c, x):
            return yhi[k, c, x + 1, one, :]

        here = [xlo[k, f, c] for c in range(3)]
        lam = lame[0]
        mu = shear[0]
        after = [state[f, c, 0] for c in range(3)]
        across = [next_y(here[c], row(c, -1)) for c in range(2)]
        along = [next_z(here[c]) for c in (0, 2)]
        xx = after[0] - here[0]
        dilation = xx + (across[1] - here[1]) + (along[1] - here[2])
        low = [
            lam * dilation + 2.0 * mu * xx,
            mu * ((across[0] - here[0]) + (after[1] - here[1])),
            mu * ((along[0] - here[0]) + (after[2] - here[2])),
        ]
        cell = cells[f]
        amp = [amps[(f * STEPS + k) * 3 + c] for c in range(3)]
        for x in range(cells_x):
            here = after
            after = [state[f, c, x + 1] if x < last else xhi[k, f, c] for c in range(3)]
            lam = lame[x + 1]
            mu = shear[x + 1]
            twice = 2.0 * mu
            gx_ = [after[c] - here[c] for c in range(3)]
            gy_ = [next_y(here[c], row(c, x)) - here[c] for c in range(3)]
            gz_ = [next_z(here[c]) - here[c] for c in range(3)]
            spread = lam * (gx_[0] + gy_[1] + gz_[2])
            xx = spread + twice * gx_[0]
            yy = spread + twice * gy_[1]
            zz = spread + twice * gz_[2]
            xy = mu * (gy_[0] + gx_[1])
            xz = mu * (gz_[0] + gx_[2])
            yz = mu * (gz_[1] + gy_[2])
            wall_xy, wall_yy, wall_yz = [low_stress[k, j, x, one, :] for j in range(3)]
            force = [
                (xx - low[0]) + (xy - last_y(xy, wall_xy)) + (xz - last_z(xz)),
                (xy - low[1]) + (yy - last_y(yy, wall_yy)) + (yz - last_z(yz)),
                (xz - low[2]) + (yz - last_y(yz, wall_yz)) + (zz - last_z(zz)),
            ]
            low = [xx, xy, xz]
            placed = flat_at == cell - (first_cell + x * plane_cells)
            scaled = time_step_sq * buoy[x]
            for c in range(3):
                moved = force[c] + jnp.where(placed, amp[c], 0.0)
                put(f, c, x, 2.0 * here[c] - earlier[f, c, x] + scaled * moved)

    def strain(planes, rows):
        for x in range(cells_x):
            here, after = planes[x], planes[x + 1]
            gx_ = [after[c] - here[c] for c in range(3)]
            gy_ = [next_y(here[c], rows[x][c]) - here[c] for c in range(3)]
            gz_ = [next_z(here[c]) - here[c] for c in range(3)]
            yield (
                gx_[0],
                gy_[1],
                gz_[2],
                gy_[0] + gx_[1],
                gz_[0] + gx_[2],
                gz_[1] + gy_[2],
            )

    def correlate(k, state):
        def summed(load):
            total = load(0)
            for f in range(1, receivers):
                total = total + load(f)
            return total

        whole, master = [], []
        for x in range(cells_x + 1):
            if x < cells_x:
                whole.append([summed(lambda f: state[f, c, x]) for c in range(3)])
                master.append([state[receivers, c, x] for c in range(3)])
            else:
                whole.append([summed(lambda f: xhi[k, f, c]) for c in range(3)])
                master.append([xhi[k, receivers, c] for c in range(3)])
        whole_rows = [
            [summed(lambda f: yhi[k, c, x + 1, f : f + 1, :]) for c in range(3)]
            for x in range(cells_x)
        ]
        master_rows = [
            [yhi[k, c, x + 1, receivers : receivers + 1, :] for c in range(3)]
            for x in range(cells_x)
        ]
        pairs = zip(strain(whole, whole_rows), strain(master, master_rows))
        for x, (a, b) in enumerate(pairs):
            swell = (a[0] + a[1] + a[2]) * (b[0] + b[1] + b[2])
            twist = 2.0 * (a[0] * b[0] + a[1] * b[1] + a[2] * b[2])
            twist = twist + (a[3] * b[3] + a[4] * b[4] + a[5] * b[5])
            if k == 0:
                totals[0, x] = swell
                totals[1, x] = twist
            else:
                totals[0, x] += swell
                totals[1, x] += twist

    arrive(first_moduli)
    arrive(first_rows)
    wall(0)
    arrive(first_x)

    def put_mid(f, c, x, value):
        mid[f, c, x] = value
        row_first[1, c, x, f : f + 1, :] = value[0:1]
        row_last[1, c, x, f : f + 1, :] = value[cells_y - 1 : cells_y]

    for f in range(split):
        step(0, f, now, prev, put_mid)
    second_x = [
        (remote(mid.at[group, :, 0], xhi.at[1, group], down), has_down, has_up),
        (remote(mid.at[group, :, last], xlo.at[1, group], up), has_up, has_down),
    ]
    start(second_x)
    arrive(first_rest)
    for f in range(split, fields):
        step(0, f, now, prev, put_mid)
    second_rest = [
        (remote(mid.at[rest_all, :, 0], xhi.at[1, rest_all], down), has_down, has_up),
        (remote(mid.at[rest_all, :, last], xlo.at[1, rest_all], up), has_up, has_down),
    ]
    second_rows = rows(1)
    start(second_rest)
    start(second_rows)
    second_round = second_x + second_rest + second_rows
    correlate(0, now)
    arrive(second_round)
    correlate(1, mid)

    share = depth // groups
    lane_part = lane_at // share
    for g in range(groups):
        for j in range(2):
            packed = None
            for x in range(cells_x):
                turn = (share * (x - g)) % depth
                piece = totals[j, x] if turn == 0 else pltpu.roll(totals[j, x], turn, 1)
                packed = piece if packed is None else jnp.where(lane_part == x, piece, packed)
            share_send[g, j] = packed
    third_round = [
        (remote(share_send.at[peers[d][0]], share_recv.at[d], peers[d]), True, True)
        for d in range(groups - 1)
    ]
    for copy, _, _ in third_round:
        copy.start()

    def put_out(f, c, x, value):
        adj_out[f, c, x] = value

    wall(1)
    for f in range(receivers):
        step(1, f, mid, now, put_out)

    for copy, _, _ in third_round:
        copy.wait_recv()
    scale_out = 1.0 / (STEPS * receivers * groups)
    for j in range(2):
        part = share_send[grp, j]
        for d in range(groups - 1):
            part = part + share_recv[d, j]
        part = part * scale_out
        for x in range(cells_x):
            piece = part if x == 0 else pltpu.roll(part, depth - share * x, 1)
            kern_out[j, x] = piece[:, 0:share]
    sent(first_x + first_moduli + first_rest + first_rows)
    sent(second_round)
    for copy, _, _ in third_round:
        copy.wait_send()


def local(
    fwd_now,
    fwd_prev,
    adj_now,
    adj_prev,
    lame_first,
    shear_mod,
    buoyancy,
    master_cell,
    master_lag,
    master_trace,
    receiver_cell,
    receiver_lag,
    receiver_trace,
):
    cells_x, cells_y, depth = lame_first.shape
    receivers = adj_now.shape[0]
    fields = receivers + 1
    sizes = tuple(lax.axis_size(axis) for axis in ("grp", "gx", "gy"))
    groups = sizes[0]
    lanes = -(-fields // 8) * 8
    block = (fields, 3, cells_x, cells_y, depth)
    scalar = pl.BlockSpec(memory_space=pltpu.SMEM)
    whole = pl.BlockSpec(memory_space=pltpu.HBM)
    vector = pl.BlockSpec(memory_space=pltpu.VMEM)

    def room(*shape):
        return pltpu.VMEM(shape, jnp.float32)

    def stay(value):
        return pltpu.with_memory_space_constraint(value, pltpu.HBM)

    return pl.pallas_call(
        functools.partial(kernel, sizes),
        out_shape=(
            pltpu.VMEM(adj_now.shape, jnp.float32),
            pltpu.VMEM((2, cells_x, cells_y, depth // groups), jnp.float32),
        ),
        in_specs=[scalar] * 2 + [whole] * 11,
        out_specs=(vector, vector),
        scratch_shapes=[
            room(*block),
            room(*block),
            room(*block),
            room(cells_x + 1, cells_y, depth),
            room(cells_x + 1, cells_y, depth),
            room(cells_x, cells_y, depth),
            room(STEPS, fields, 3, cells_y, depth),
            room(STEPS, fields, 3, cells_y, depth),
            room(STEPS, 3, cells_x + 1, lanes, depth),
            room(STEPS, 3, cells_x + 1, lanes, depth),
            room(STEPS, 3, cells_x, lanes, depth),
            room(STEPS, 3, cells_x, lanes, depth),
            room(2 * cells_x, depth),
            room(2 * cells_x, depth),
            room(STEPS, 3, cells_x, lanes, depth),
            room(2, cells_x, cells_y, depth),
            room(groups, 2, cells_y, depth),
            room(groups - 1, 2, cells_y, depth),
            pltpu.SMEM((fields,), jnp.int32),
            pltpu.SMEM((fields * STEPS * 3,), jnp.float32),
            pltpu.SMEM((3,) + master_trace.shape[:1], jnp.float32),
            pltpu.SMEM((receivers,), jnp.int32),
            pltpu.SMEM((receivers,), jnp.int32),
            pltpu.SMEM((3,) + receiver_trace.shape[:2], jnp.float32),
            pltpu.SemaphoreType.DMA((11,)),
            pltpu.SemaphoreType.DMA((32,)),
            pltpu.SemaphoreType.DMA((32,)),
        ],
        compiler_params=pltpu.CompilerParams(
            collective_id=0, has_side_effects=True, vmem_limit_bytes=32 * 1024 * 1024
        ),
    )(
        master_cell,
        master_lag,
        stay(master_trace.T),
        stay(receiver_cell),
        stay(receiver_lag),
        stay(receiver_trace.transpose(2, 0, 1)),
        stay(fwd_now),
        stay(fwd_prev),
        stay(adj_now),
        stay(adj_prev),
        stay(lame_first),
        stay(shear_mod),
        stay(buoyancy),
    )


def solution(mesh):
    in_specs = (
        P(None, "gx", "gy", None),
        P(None, "gx", "gy", None),
        P("grp", None, "gx", "gy", None),
        P("grp", None, "gx", "gy", None),
        P("gx", "gy", None),
        P("gx", "gy", None),
        P("gx", "gy", None),
        P(),
        P(),
        P(),
        P("grp"),
        P("grp"),
        P("grp", None, None),
    )
    out_specs = (P("grp", None, "gx", "gy", None), P(None, "gx", "gy", "grp"))
    return jax.shard_map(local, mesh=mesh, in_specs=in_specs, out_specs=out_specs, check_vma=False)
```

```python
import functools

import jax
import jax.numpy as jnp
from jax import lax
from jax.experimental import pallas as pl
from jax.experimental.pallas import tpu as pltpu
from jax.sharding import PartitionSpec as P

STEPS = 2
MESH = pl.DeviceIdType.MESH

time_step_sq = 0.0625


def kernel(
    sizes,
    master_cell,
    master_lag,
    master_trace,
    receiver_cell,
    receiver_lag,
    receiver_trace,
    fwd_now,
    fwd_prev,
    adj_now,
    adj_prev,
    lame_first,
    shear_mod,
    buoyancy,
    adj_out,
    kern_out,
    now,
    prev,
    mid,
    lame,
    shear,
    buoy,
    xlo,
    xhi,
    ylo,
    yhi,
    row_first,
    row_last,
    mod_send,
    mod_recv,
    low_stress,
    totals,
    share_send,
    share_recv,
    cells,
    amps,
    master_trace_s,
    receiver_cell_s,
    receiver_lag_s,
    receiver_trace_s,
    load_sem,
    send_sem,
    recv_sem,
):
    groups, count_x, count_y = sizes
    receivers, _, cells_x, cells_y, depth = adj_now.shape
    fields = receivers + 1
    grp = lax.axis_index("grp")
    gx = lax.axis_index("gx")
    gy = lax.axis_index("gy")
    has_down = gx > 0
    has_up = gx < count_x - 1
    has_left = gy > 0
    has_right = gy < count_y - 1
    corner_ul = jnp.logical_and(has_up, has_left)
    corner_dr = jnp.logical_and(has_down, has_right)
    down = (grp, gx - 1, gy)
    up = (grp, gx + 1, gy)
    left = (grp, gx, gy - 1)
    right = (grp, gx, gy + 1)
    up_left = (grp, gx + 1, gy - 1)
    down_right = (grp, gx - 1, gy + 1)
    peers = [(lax.rem(grp + d, groups), gx, gy) for d in range(1, groups)]
    sides = (
        (has_down, down),
        (has_up, up),
        (has_left, left),
        (has_right, right),
        (corner_ul, up_left),
        (corner_dr, down_right),
    )

    loads = [
        (adj_now, now.at[pl.ds(0, receivers)]),
        (fwd_now, now.at[receivers]),
        (lame_first, lame.at[pl.ds(1, cells_x)]),
        (shear_mod, shear.at[pl.ds(1, cells_x)]),
        (adj_prev, prev.at[pl.ds(0, receivers)]),
        (fwd_prev, prev.at[receivers]),
        (buoyancy, buoy),
        (master_trace, master_trace_s),
        (receiver_cell, receiver_cell_s),
        (receiver_lag, receiver_lag_s),
        (receiver_trace, receiver_trace_s),
    ]
    loads = [pltpu.make_async_copy(src, dst, load_sem.at[i]) for i, (src, dst) in enumerate(loads)]
    for copy in loads:
        copy.start()

    barrier = pltpu.get_barrier_semaphore()
    expected = jnp.int32(groups - 1)
    for there, where in sides:
        expected = expected + there.astype(jnp.int32)

        @pl.when(there)
        def _():
            pl.semaphore_signal(barrier, inc=1, device_id=where, device_id_type=MESH)

    for where in peers:
        pl.semaphore_signal(barrier, inc=1, device_id=where, device_id_type=MESH)

    @pl.when(jnp.logical_not(has_down))
    def _():
        xlo[...] = jnp.zeros_like(xlo)
        lame[0] = jnp.zeros_like(lame[0])
        shear[0] = jnp.zeros_like(shear[0])

    @pl.when(jnp.logical_not(has_up))
    def _():
        xhi[...] = jnp.zeros_like(xhi)

    @pl.when(jnp.logical_not(has_left))
    def _():
        ylo[:, :, 0:cells_x] = jnp.zeros_like(ylo[:, :, 0:cells_x])
        mod_recv[...] = jnp.zeros_like(mod_recv)

    @pl.when(jnp.logical_not(has_right))
    def _():
        yhi[:, :, 1 : cells_x + 1] = jnp.zeros_like(yhi[:, :, 1 : cells_x + 1])

    @pl.when(jnp.logical_not(corner_ul))
    def _():
        ylo[:, :, cells_x] = jnp.zeros_like(ylo[:, :, cells_x])

    @pl.when(jnp.logical_not(corner_dr))
    def _():
        yhi[:, :, 0] = jnp.zeros_like(yhi[:, :, 0])

    row_first[...] = jnp.zeros_like(row_first)
    row_last[...] = jnp.zeros_like(row_last)

    pl.semaphore_wait(barrier, expected)

    number = [0]

    def remote(src, dst, where):
        i = number[0]
        number[0] += 1
        return pltpu.make_async_remote_copy(
            src_ref=src,
            dst_ref=dst,
            send_sem=send_sem.at[i],
            recv_sem=recv_sem.at[i],
            device_id=where,
            device_id_type=MESH,
        )

    def rows(k):
        return [
            (remote(row_first.at[k, :, cells_x - 1], yhi.at[k, :, 0], up_left), corner_ul, corner_dr),
            (remote(row_last.at[k, :, 0], ylo.at[k, :, cells_x], down_right), corner_dr, corner_ul),
            (remote(row_first.at[k], yhi.at[k, :, pl.ds(1, cells_x)], left), has_left, has_right),
            (remote(row_last.at[k], ylo.at[k, :, pl.ds(0, cells_x)], right), has_right, has_left),
        ]

    def start(copies):
        for copy, sends, _ in copies:
            pl.when(sends)(copy.start)

    def arrive(copies):
        for copy, _, gets in copies:
            pl.when(gets)(copy.wait_recv)

    def sent(copies):
        for copy, sends, _ in copies:
            pl.when(sends)(copy.wait_send)

    last = cells_x - 1
    split = (receivers + 2) // 2
    group = pl.ds(0, split)
    rest = pl.ds(split, receivers - split)
    rest_all = pl.ds(split, fields - split)
    first_x = [
        (remote(adj_now.at[group, :, 0], xhi.at[0, group], down), has_down, has_up),
        (remote(adj_now.at[group, :, last], xlo.at[0, group], up), has_up, has_down),
    ]
    first_moduli = [
        (remote(lame_first.at[last], lame.at[0], up), has_up, has_down),
        (remote(shear_mod.at[last], shear.at[0], up), has_up, has_down),
        (remote(mod_send, mod_recv, right), has_right, has_left),
    ]
    first_rest = [
        (remote(adj_now.at[rest, :, 0], xhi.at[0, rest], down), has_down, has_up),
        (remote(adj_now.at[rest, :, last], xlo.at[0, rest], up), has_up, has_down),
        (remote(fwd_now.at[:, 0], xhi.at[0, receivers], down), has_down, has_up),
        (remote(fwd_now.at[:, last], xlo.at[0, receivers], up), has_up, has_down),
    ]
    first_rows = rows(0)
    start(first_moduli[:2])
    start(first_x)
    start(first_rest)

    for copy in loads[:4]:
        copy.wait()

    for f in range(fields):
        for c in range(3):
            for x in range(cells_x):
                row_first[0, c, x, f : f + 1, :] = now[f, c, x, 0:1, :]
                row_last[0, c, x, f : f + 1, :] = now[f, c, x, cells_y - 1 : cells_y, :]
    for x in range(cells_x):
        mod_send[x : x + 1] = lame[x + 1, cells_y - 1 : cells_y, :]
        mod_send[cells_x + x : cells_x + x + 1] = shear[x + 1, cells_y - 1 : cells_y, :]

    start(first_rows)
    start(first_moduli[2:])

    for copy in loads[4:]:
        copy.wait()

    for f in range(fields):
        master = f == receivers
        cells[f] = master_cell[0] if master else receiver_cell_s[f]
        lag = master_lag[0] if master else receiver_lag_s[f]
        for k in range(STEPS):
            for c in range(3):
                spot = (f * STEPS + k) * 3 + c
                amps[spot] = master_trace_s[c, lag + k] if master else receiver_trace_s[c, f, lag + k]

    row_at = lax.broadcasted_iota(jnp.int32, (cells_y, depth), 0)
    lane_at = lax.broadcasted_iota(jnp.int32, (cells_y, depth), 1)
    flat_at = row_at * depth + lane_at
    top = row_at == 0
    bottom = row_at == cells_y - 1
    front = lane_at == 0
    back = lane_at == depth - 1
    plane_cells = cells_y * count_y * depth
    first_cell = gx * cells_x * plane_cells + gy * cells_y * depth

    def next_z(v):
        return jnp.where(back, 0.0, pltpu.roll(v, depth - 1, 1))

    def last_z(v):
        return jnp.where(front, 0.0, pltpu.roll(v, 1, 1))

    def next_y(v, row):
        return jnp.where(bottom, row, pltpu.roll(v, cells_y - 1, 0))

    def last_y(v, row):
        return jnp.where(top, row, pltpu.roll(v, 1, 0))

    def wall(k):
        for x in range(cells_x):
            here = [ylo[k, c, x] for c in range(3)]
            beside = [ylo[k, c, x + 1] for c in range(3)]
            above = [row_first[k, c, x] for c in range(3)]
            lam = mod_recv[x : x + 1]
            mu = mod_recv[cells_x + x : cells_x + x + 1]
            grad_y = [above[c] - here[c] for c in range(3)]
            xy = grad_y[0] + (beside[1] - here[1])
            yz = (next_z(here[1]) - here[1]) + grad_y[2]
            dilation = (beside[0] - here[0]) + grad_y[1] + (next_z(here[2]) - here[2])
            low_stress[k, 0, x] = mu * xy
            low_stress[k, 1, x] = lam * dilation + 2.0 * mu * grad_y[1]
            low_stress[k, 2, x] = mu * yz

    def step(k, f, state, earlier, put):
        one = slice(f, f + 1)

        def row(c, x):
            return yhi[k, c, x + 1, one, :]

        here = [xlo[k, f, c] for c in range(3)]
        lam = lame[0]
        mu = shear[0]
        after = [state[f, c, 0] for c in range(3)]
        across = [next_y(here[c], row(c, -1)) for c in range(2)]
        along = [next_z(here[c]) for c in (0, 2)]
        xx = after[0] - here[0]
        dilation = xx + (across[1] - here[1]) + (along[1] - here[2])
        low = [
            lam * dilation + 2.0 * mu * xx,
            mu * ((across[0] - here[0]) + (after[1] - here[1])),
            mu * ((along[0] - here[0]) + (after[2] - here[2])),
        ]
        cell = cells[f]
        amp = [amps[(f * STEPS + k) * 3 + c] for c in range(3)]
        for x in range(cells_x):
            here = after
            after = [state[f, c, x + 1] if x < last else xhi[k, f, c] for c in range(3)]
            lam = lame[x + 1]
            mu = shear[x + 1]
            twice = 2.0 * mu
            gx_ = [after[c] - here[c] for c in range(3)]
            gy_ = [next_y(here[c], row(c, x)) - here[c] for c in range(3)]
            gz_ = [next_z(here[c]) - here[c] for c in range(3)]
            spread = lam * (gx_[0] + gy_[1] + gz_[2])
            xx = spread + twice * gx_[0]
            yy = spread + twice * gy_[1]
            zz = spread + twice * gz_[2]
            xy = mu * (gy_[0] + gx_[1])
            xz = mu * (gz_[0] + gx_[2])
            yz = mu * (gz_[1] + gy_[2])
            wall_xy, wall_yy, wall_yz = [low_stress[k, j, x, one, :] for j in range(3)]
            force = [
                (xx - low[0]) + (xy - last_y(xy, wall_xy)) + (xz - last_z(xz)),
                (xy - low[1]) + (yy - last_y(yy, wall_yy)) + (yz - last_z(yz)),
                (xz - low[2]) + (yz - last_y(yz, wall_yz)) + (zz - last_z(zz)),
            ]
            low = [xx, xy, xz]
            placed = flat_at == cell - (first_cell + x * plane_cells)
            scaled = time_step_sq * buoy[x]
            for c in range(3):
                moved = force[c] + jnp.where(placed, amp[c], 0.0)
                put(f, c, x, 2.0 * here[c] - earlier[f, c, x] + scaled * moved)

    def strain(planes, rows):
        for x in range(cells_x):
            here, after = planes[x], planes[x + 1]
            gx_ = [after[c] - here[c] for c in range(3)]
            gy_ = [next_y(here[c], rows[x][c]) - here[c] for c in range(3)]
            gz_ = [next_z(here[c]) - here[c] for c in range(3)]
            yield (
                gx_[0],
                gy_[1],
                gz_[2],
                gy_[0] + gx_[1],
                gz_[0] + gx_[2],
                gz_[1] + gy_[2],
            )

    def correlate(k, state):
        def summed(load):
            total = load(0)
            for f in range(1, receivers):
                total = total + load(f)
            return total

        whole, master = [], []
        for x in range(cells_x + 1):
            if x < cells_x:
                whole.append([summed(lambda f: state[f, c, x]) for c in range(3)])
                master.append([state[receivers, c, x] for c in range(3)])
            else:
                whole.append([summed(lambda f: xhi[k, f, c]) for c in range(3)])
                master.append([xhi[k, receivers, c] for c in range(3)])
        whole_rows = [
            [summed(lambda f: yhi[k, c, x + 1, f : f + 1, :]) for c in range(3)]
            for x in range(cells_x)
        ]
        master_rows = [
            [yhi[k, c, x + 1, receivers : receivers + 1, :] for c in range(3)]
            for x in range(cells_x)
        ]
        pairs = zip(strain(whole, whole_rows), strain(master, master_rows))
        for x, (a, b) in enumerate(pairs):
            swell = (a[0] + a[1] + a[2]) * (b[0] + b[1] + b[2])
            twist = 2.0 * (a[0] * b[0] + a[1] * b[1] + a[2] * b[2])
            twist = twist + (a[3] * b[3] + a[4] * b[4] + a[5] * b[5])
            if k == 0:
                totals[0, x] = swell
                totals[1, x] = twist
            else:
                totals[0, x] += swell
                totals[1, x] += twist

    arrive(first_moduli)
    arrive(first_rows)
    wall(0)
    arrive(first_x)

    def put_mid(f, c, x, value):
        mid[f, c, x] = value
        row_first[1, c, x, f : f + 1, :] = value[0:1]
        row_last[1, c, x, f : f + 1, :] = mid[f, c, x, cells_y - 1 : cells_y, :]

    for f in range(split):
        step(0, f, now, prev, put_mid)
    second_x = [
        (remote(mid.at[group, :, 0], xhi.at[1, group], down), has_down, has_up),
        (remote(mid.at[group, :, last], xlo.at[1, group], up), has_up, has_down),
    ]
    start(second_x)
    arrive(first_rest)
    for f in range(split, fields):
        step(0, f, now, prev, put_mid)
    second_rest = [
        (remote(mid.at[rest_all, :, 0], xhi.at[1, rest_all], down), has_down, has_up),
        (remote(mid.at[rest_all, :, last], xlo.at[1, rest_all], up), has_up, has_down),
    ]
    second_rows = rows(1)
    start(second_rest)
    start(second_rows)
    second_round = second_x + second_rest + second_rows
    correlate(0, now)
    arrive(second_round)
    correlate(1, mid)

    share = depth // groups
    lane_part = lane_at // share
    for g in range(groups):
        for j in range(2):
            packed = None
            for x in range(cells_x):
                turn = (share * (x - g)) % depth
                piece = totals[j, x] if turn == 0 else pltpu.roll(totals[j, x], turn, 1)
                packed = piece if packed is None else jnp.where(lane_part == x, piece, packed)
            share_send[g, j] = packed
    third_round = [
        (remote(share_send.at[peers[d][0]], share_recv.at[d], peers[d]), True, True)
        for d in range(groups - 1)
    ]
    for copy, _, _ in third_round:
        copy.start()

    def put_out(f, c, x, value):
        adj_out[f, c, x] = value

    wall(1)
    for f in range(receivers):
        step(1, f, mid, now, put_out)

    for copy, _, _ in third_round:
        copy.wait_recv()
    scale_out = 1.0 / (STEPS * receivers * groups)
    for j in range(2):
        part = share_send[grp, j]
        for d in range(groups - 1):
            part = part + share_recv[d, j]
        part = part * scale_out
        for x in range(cells_x):
            piece = part if x == 0 else pltpu.roll(part, depth - share * x, 1)
            kern_out[j, x] = piece[:, 0:share]
    sent(first_x + first_moduli + first_rest + first_rows)
    sent(second_round)
    for copy, _, _ in third_round:
        copy.wait_send()


def hand_over(adj_made, kern_made, adj_out, kern_out, sems):
    adj_copy = pltpu.make_async_copy(adj_made, adj_out, sems.at[0])
    kern_copy = pltpu.make_async_copy(kern_made, kern_out, sems.at[1])
    adj_copy.start()
    kern_copy.start()
    adj_copy.wait()
    kern_copy.wait()


def local(
    fwd_now,
    fwd_prev,
    adj_now,
    adj_prev,
    lame_first,
    shear_mod,
    buoyancy,
    master_cell,
    master_lag,
    master_trace,
    receiver_cell,
    receiver_lag,
    receiver_trace,
):
    cells_x, cells_y, depth = lame_first.shape
    receivers = adj_now.shape[0]
    fields = receivers + 1
    sizes = tuple(lax.axis_size(axis) for axis in ("grp", "gx", "gy"))
    groups = sizes[0]
    lanes = -(-fields // 8) * 8
    block = (fields, 3, cells_x, cells_y, depth)
    scalar = pl.BlockSpec(memory_space=pltpu.SMEM)
    whole = pl.BlockSpec(memory_space=pltpu.HBM)
    vector = pl.BlockSpec(memory_space=pltpu.VMEM)

    def room(*shape):
        return pltpu.VMEM(shape, jnp.float32)

    def stay(value):
        return pltpu.with_memory_space_constraint(value, pltpu.HBM)

    made = pl.pallas_call(
        functools.partial(kernel, sizes),
        out_shape=(
            pltpu.VMEM(adj_now.shape, jnp.float32),
            pltpu.VMEM((2, cells_x, cells_y, depth // groups), jnp.float32),
        ),
        in_specs=[scalar] * 2 + [whole] * 11,
        out_specs=(vector, vector),
        scratch_shapes=[
            room(*block),
            room(*block),
            room(*block),
            room(cells_x + 1, cells_y, depth),
            room(cells_x + 1, cells_y, depth),
            room(cells_x, cells_y, depth),
            room(STEPS, fields, 3, cells_y, depth),
            room(STEPS, fields, 3, cells_y, depth),
            room(STEPS, 3, cells_x + 1, lanes, depth),
            room(STEPS, 3, cells_x + 1, lanes, depth),
            room(STEPS, 3, cells_x, lanes, depth),
            room(STEPS, 3, cells_x, lanes, depth),
            room(2 * cells_x, depth),
            room(2 * cells_x, depth),
            room(STEPS, 3, cells_x, lanes, depth),
            room(2, cells_x, cells_y, depth),
            room(groups, 2, cells_y, depth),
            room(groups - 1, 2, cells_y, depth),
            pltpu.SMEM((fields,), jnp.int32),
            pltpu.SMEM((fields * STEPS * 3,), jnp.float32),
            pltpu.SMEM((3,) + master_trace.shape[:1], jnp.float32),
            pltpu.SMEM((receivers,), jnp.int32),
            pltpu.SMEM((receivers,), jnp.int32),
            pltpu.SMEM((3,) + receiver_trace.shape[:2], jnp.float32),
            pltpu.SemaphoreType.DMA((11,)),
            pltpu.SemaphoreType.DMA((32,)),
            pltpu.SemaphoreType.DMA((32,)),
        ],
        compiler_params=pltpu.CompilerParams(
            collective_id=0, has_side_effects=True, vmem_limit_bytes=32 * 1024 * 1024
        ),
    )(
        master_cell,
        master_lag,
        stay(master_trace.T),
        stay(receiver_cell),
        stay(receiver_lag),
        stay(receiver_trace.transpose(2, 0, 1)),
        stay(fwd_now),
        stay(fwd_prev),
        stay(adj_now),
        stay(adj_prev),
        stay(lame_first),
        stay(shear_mod),
        stay(buoyancy),
    )
    made = [pltpu.with_memory_space_constraint(value, pltpu.VMEM) for value in made]
    return pl.pallas_call(
        hand_over,
        out_shape=tuple(jax.ShapeDtypeStruct(value.shape, value.dtype) for value in made),
        in_specs=[pl.BlockSpec(memory_space=pltpu.VMEM)] * 2,
        out_specs=(whole, whole),
        scratch_shapes=[pltpu.SemaphoreType.DMA((2,))],
    )(*made)


def solution(mesh):
    in_specs = (
        P(None, "gx", "gy", None),
        P(None, "gx", "gy", None),
        P("grp", None, "gx", "gy", None),
        P("grp", None, "gx", "gy", None),
        P("gx", "gy", None),
        P("gx", "gy", None),
        P("gx", "gy", None),
        P(),
        P(),
        P(),
        P("grp"),
        P("grp"),
        P("grp", None, None),
    )
    out_specs = (P("grp", None, "gx", "gy", None), P(None, "gx", "gy", "grp"))
    return jax.shard_map(local, mesh=mesh, in_specs=in_specs, out_specs=out_specs, check_vma=False)
```

```python
import functools

import jax
import jax.numpy as jnp
from jax import lax
from jax.experimental import pallas as pl
from jax.experimental.pallas import tpu as pltpu
from jax.sharding import PartitionSpec as P

STEPS = 2
MESH = pl.DeviceIdType.MESH

time_step_sq = 0.0625


def kernel(
    sizes,
    master_cell,
    master_lag,
    master_trace,
    receiver_cell,
    receiver_lag,
    receiver_trace,
    fwd_now,
    fwd_prev,
    adj_now,
    adj_prev,
    lame_first,
    shear_mod,
    buoyancy,
    adj_out,
    kern_out,
    now,
    prev,
    mid,
    lame,
    shear,
    buoy,
    xlo,
    xhi,
    ylo,
    yhi,
    row_first,
    row_last,
    mod_send,
    mod_recv,
    low_stress,
    totals,
    share_send,
    share_recv,
    cells,
    amps,
    master_trace_s,
    receiver_cell_s,
    receiver_lag_s,
    receiver_trace_s,
    load_sem,
    send_sem,
    recv_sem,
):
    groups, count_x, count_y = sizes
    receivers, _, cells_x, cells_y, depth = adj_now.shape
    fields = receivers + 1
    grp = lax.axis_index("grp")
    gx = lax.axis_index("gx")
    gy = lax.axis_index("gy")
    has_down = gx > 0
    has_up = gx < count_x - 1
    has_left = gy > 0
    has_right = gy < count_y - 1
    corner_ul = jnp.logical_and(has_up, has_left)
    corner_dr = jnp.logical_and(has_down, has_right)
    down = (grp, gx - 1, gy)
    up = (grp, gx + 1, gy)
    left = (grp, gx, gy - 1)
    right = (grp, gx, gy + 1)
    up_left = (grp, gx + 1, gy - 1)
    down_right = (grp, gx - 1, gy + 1)
    peers = [(lax.rem(grp + d, groups), gx, gy) for d in range(1, groups)]
    sides = (
        (has_down, down),
        (has_up, up),
        (has_left, left),
        (has_right, right),
        (corner_ul, up_left),
        (corner_dr, down_right),
    )

    barrier = pltpu.get_barrier_semaphore()
    expected = jnp.int32(groups - 1)
    for there, where in sides:
        expected = expected + there.astype(jnp.int32)

        @pl.when(there)
        def _():
            pl.semaphore_signal(barrier, inc=1, device_id=where, device_id_type=MESH)

    for where in peers:
        pl.semaphore_signal(barrier, inc=1, device_id=where, device_id_type=MESH)

    loads = [
        (adj_now, now.at[pl.ds(0, receivers)]),
        (fwd_now, now.at[receivers]),
        (lame_first, lame.at[pl.ds(1, cells_x)]),
        (shear_mod, shear.at[pl.ds(1, cells_x)]),
        (adj_prev, prev.at[pl.ds(0, receivers)]),
        (fwd_prev, prev.at[receivers]),
        (buoyancy, buoy),
        (master_trace, master_trace_s),
        (receiver_cell, receiver_cell_s),
        (receiver_lag, receiver_lag_s),
        (receiver_trace, receiver_trace_s),
    ]
    loads = [pltpu.make_async_copy(src, dst, load_sem.at[i]) for i, (src, dst) in enumerate(loads)]
    for copy in loads:
        copy.start()

    pl.semaphore_wait(barrier, expected)

    number = [0]

    def remote(src, dst, where):
        i = number[0]
        number[0] += 1
        return pltpu.make_async_remote_copy(
            src_ref=src,
            dst_ref=dst,
            send_sem=send_sem.at[i],
            recv_sem=recv_sem.at[i],
            device_id=where,
            device_id_type=MESH,
        )

    def rows(k):
        return [
            (remote(row_first.at[k, :, cells_x - 1], yhi.at[k, :, 0], up_left), corner_ul, corner_dr),
            (remote(row_last.at[k, :, 0], ylo.at[k, :, cells_x], down_right), corner_dr, corner_ul),
            (remote(row_first.at[k], yhi.at[k, :, pl.ds(1, cells_x)], left), has_left, has_right),
            (remote(row_last.at[k], ylo.at[k, :, pl.ds(0, cells_x)], right), has_right, has_left),
        ]

    def start(copies):
        for copy, sends, _ in copies:
            pl.when(sends)(copy.start)

    def arrive(copies):
        for copy, _, gets in copies:
            pl.when(gets)(copy.wait_recv)

    def sent(copies):
        for copy, sends, _ in copies:
            pl.when(sends)(copy.wait_send)

    last = cells_x - 1
    split = (receivers + 2) // 2
    group = pl.ds(0, split)
    rest = pl.ds(split, receivers - split)
    rest_all = pl.ds(split, fields - split)
    first_x = [
        (remote(adj_now.at[group, :, 0], xhi.at[0, group], down), has_down, has_up),
        (remote(adj_now.at[group, :, last], xlo.at[0, group], up), has_up, has_down),
    ]
    first_moduli = [
        (remote(lame_first.at[last], lame.at[0], up), has_up, has_down),
        (remote(shear_mod.at[last], shear.at[0], up), has_up, has_down),
        (remote(mod_send, mod_recv, right), has_right, has_left),
    ]
    first_rest = [
        (remote(adj_now.at[rest, :, 0], xhi.at[0, rest], down), has_down, has_up),
        (remote(adj_now.at[rest, :, last], xlo.at[0, rest], up), has_up, has_down),
        (remote(fwd_now.at[:, 0], xhi.at[0, receivers], down), has_down, has_up),
        (remote(fwd_now.at[:, last], xlo.at[0, receivers], up), has_up, has_down),
    ]
    first_rows = rows(0)
    start(first_moduli[:2])
    start(first_x)
    start(first_rest)

    @pl.when(jnp.logical_not(has_down))
    def _():
        xlo[...] = jnp.zeros_like(xlo)
        lame[0] = jnp.zeros_like(lame[0])
        shear[0] = jnp.zeros_like(shear[0])

    @pl.when(jnp.logical_not(has_up))
    def _():
        xhi[...] = jnp.zeros_like(xhi)

    @pl.when(jnp.logical_not(has_left))
    def _():
        ylo[:, :, 0:cells_x] = jnp.zeros_like(ylo[:, :, 0:cells_x])
        mod_recv[...] = jnp.zeros_like(mod_recv)

    @pl.when(jnp.logical_not(has_right))
    def _():
        yhi[:, :, 1 : cells_x + 1] = jnp.zeros_like(yhi[:, :, 1 : cells_x + 1])

    @pl.when(jnp.logical_not(corner_ul))
    def _():
        ylo[:, :, cells_x] = jnp.zeros_like(ylo[:, :, cells_x])

    @pl.when(jnp.logical_not(corner_dr))
    def _():
        yhi[:, :, 0] = jnp.zeros_like(yhi[:, :, 0])

    row_first[...] = jnp.zeros_like(row_first)
    row_last[...] = jnp.zeros_like(row_last)

    for copy in loads[:4]:
        copy.wait()

    for f in range(fields):
        for c in range(3):
            for x in range(cells_x):
                row_first[0, c, x, f : f + 1, :] = now[f, c, x, 0:1, :]
                row_last[0, c, x, f : f + 1, :] = now[f, c, x, cells_y - 1 : cells_y, :]
    for x in range(cells_x):
        mod_send[x : x + 1] = lame[x + 1, cells_y - 1 : cells_y, :]
        mod_send[cells_x + x : cells_x + x + 1] = shear[x + 1, cells_y - 1 : cells_y, :]

    start(first_rows)
    start(first_moduli[2:])

    for copy in loads[4:]:
        copy.wait()

    for f in range(fields):
        master = f == receivers
        cells[f] = master_cell[0] if master else receiver_cell_s[f]
        lag = master_lag[0] if master else receiver_lag_s[f]
        for k in range(STEPS):
            for c in range(3):
                spot = (f * STEPS + k) * 3 + c
                amps[spot] = master_trace_s[c, lag + k] if master else receiver_trace_s[c, f, lag + k]

    row_at = lax.broadcasted_iota(jnp.int32, (cells_y, depth), 0)
    lane_at = lax.broadcasted_iota(jnp.int32, (cells_y, depth), 1)
    flat_at = row_at * depth + lane_at
    top = row_at == 0
    bottom = row_at == cells_y - 1
    front = lane_at == 0
    back = lane_at == depth - 1
    plane_cells = cells_y * count_y * depth
    first_cell = gx * cells_x * plane_cells + gy * cells_y * depth

    def next_z(v):
        return jnp.where(back, 0.0, pltpu.roll(v, depth - 1, 1))

    def last_z(v):
        return jnp.where(front, 0.0, pltpu.roll(v, 1, 1))

    def next_y(v, row):
        return jnp.where(bottom, row, pltpu.roll(v, cells_y - 1, 0))

    def last_y(v, row):
        return jnp.where(top, row, pltpu.roll(v, 1, 0))

    def wall(k):
        for x in range(cells_x):
            here = [ylo[k, c, x] for c in range(3)]
            beside = [ylo[k, c, x + 1] for c in range(3)]
            above = [row_first[k, c, x] for c in range(3)]
            lam = mod_recv[x : x + 1]
            mu = mod_recv[cells_x + x : cells_x + x + 1]
            grad_y = [above[c] - here[c] for c in range(3)]
            xy = grad_y[0] + (beside[1] - here[1])
            yz = (next_z(here[1]) - here[1]) + grad_y[2]
            dilation = (beside[0] - here[0]) + grad_y[1] + (next_z(here[2]) - here[2])
            low_stress[k, 0, x] = mu * xy
            low_stress[k, 1, x] = lam * dilation + 2.0 * mu * grad_y[1]
            low_stress[k, 2, x] = mu * yz

    def step(k, f, state, earlier, put):
        one = slice(f, f + 1)

        def row(c, x):
            return yhi[k, c, x + 1, one, :]

        here = [xlo[k, f, c] for c in range(3)]
        lam = lame[0]
        mu = shear[0]
        after = [state[f, c, 0] for c in range(3)]
        across = [next_y(here[c], row(c, -1)) for c in range(2)]
        along = [next_z(here[c]) for c in (0, 2)]
        xx = after[0] - here[0]
        dilation = xx + (across[1] - here[1]) + (along[1] - here[2])
        low = [
            lam * dilation + 2.0 * mu * xx,
            mu * ((across[0] - here[0]) + (after[1] - here[1])),
            mu * ((along[0] - here[0]) + (after[2] - here[2])),
        ]
        cell = cells[f]
        amp = [amps[(f * STEPS + k) * 3 + c] for c in range(3)]
        for x in range(cells_x):
            here = after
            after = [state[f, c, x + 1] if x < last else xhi[k, f, c] for c in range(3)]
            lam = lame[x + 1]
            mu = shear[x + 1]
            twice = 2.0 * mu
            gx_ = [after[c] - here[c] for c in range(3)]
            gy_ = [next_y(here[c], row(c, x)) - here[c] for c in range(3)]
            gz_ = [next_z(here[c]) - here[c] for c in range(3)]
            spread = lam * (gx_[0] + gy_[1] + gz_[2])
            xx = spread + twice * gx_[0]
            yy = spread + twice * gy_[1]
            zz = spread + twice * gz_[2]
            xy = mu * (gy_[0] + gx_[1])
            xz = mu * (gz_[0] + gx_[2])
            yz = mu * (gz_[1] + gy_[2])
            wall_xy, wall_yy, wall_yz = [low_stress[k, j, x, one, :] for j in range(3)]
            force = [
                (xx - low[0]) + (xy - last_y(xy, wall_xy)) + (xz - last_z(xz)),
                (xy - low[1]) + (yy - last_y(yy, wall_yy)) + (yz - last_z(yz)),
                (xz - low[2]) + (yz - last_y(yz, wall_yz)) + (zz - last_z(zz)),
            ]
            low = [xx, xy, xz]
            placed = flat_at == cell - (first_cell + x * plane_cells)
            scaled = time_step_sq * buoy[x]
            for c in range(3):
                moved = force[c] + jnp.where(placed, amp[c], 0.0)
                put(f, c, x, 2.0 * here[c] - earlier[f, c, x] + scaled * moved)

    def strain(planes, rows):
        for x in range(cells_x):
            here, after = planes[x], planes[x + 1]
            gx_ = [after[c] - here[c] for c in range(3)]
            gy_ = [next_y(here[c], rows[x][c]) - here[c] for c in range(3)]
            gz_ = [next_z(here[c]) - here[c] for c in range(3)]
            yield (
                gx_[0],
                gy_[1],
                gz_[2],
                gy_[0] + gx_[1],
                gz_[0] + gx_[2],
                gz_[1] + gy_[2],
            )

    def correlate(k, state):
        def summed(load):
            total = load(0)
            for f in range(1, receivers):
                total = total + load(f)
            return total

        whole, master = [], []
        for x in range(cells_x + 1):
            if x < cells_x:
                whole.append([summed(lambda f: state[f, c, x]) for c in range(3)])
                master.append([state[receivers, c, x] for c in range(3)])
            else:
                whole.append([summed(lambda f: xhi[k, f, c]) for c in range(3)])
                master.append([xhi[k, receivers, c] for c in range(3)])
        whole_rows = [
            [summed(lambda f: yhi[k, c, x + 1, f : f + 1, :]) for c in range(3)]
            for x in range(cells_x)
        ]
        master_rows = [
            [yhi[k, c, x + 1, receivers : receivers + 1, :] for c in range(3)]
            for x in range(cells_x)
        ]
        pairs = zip(strain(whole, whole_rows), strain(master, master_rows))
        for x, (a, b) in enumerate(pairs):
            swell = (a[0] + a[1] + a[2]) * (b[0] + b[1] + b[2])
            twist = 2.0 * (a[0] * b[0] + a[1] * b[1] + a[2] * b[2])
            twist = twist + (a[3] * b[3] + a[4] * b[4] + a[5] * b[5])
            if k == 0:
                totals[0, x] = swell
                totals[1, x] = twist
            else:
                totals[0, x] += swell
                totals[1, x] += twist

    arrive(first_moduli)
    arrive(first_rows)
    wall(0)
    arrive(first_x)

    def put_mid(f, c, x, value):
        mid[f, c, x] = value
        row_first[1, c, x, f : f + 1, :] = value[0:1]
        row_last[1, c, x, f : f + 1, :] = mid[f, c, x, cells_y - 1 : cells_y, :]

    for f in range(split):
        step(0, f, now, prev, put_mid)
    second_x = [
        (remote(mid.at[group, :, 0], xhi.at[1, group], down), has_down, has_up),
        (remote(mid.at[group, :, last], xlo.at[1, group], up), has_up, has_down),
    ]
    start(second_x)
    arrive(first_rest)
    for f in range(split, fields):
        step(0, f, now, prev, put_mid)
    second_rest = [
        (remote(mid.at[rest_all, :, 0], xhi.at[1, rest_all], down), has_down, has_up),
        (remote(mid.at[rest_all, :, last], xlo.at[1, rest_all], up), has_up, has_down),
    ]
    second_rows = rows(1)
    start(second_rest[:1])
    start(second_rows[:3:2])
    start(second_rest[1:])
    start(second_rows[1::2])
    second_round = second_x + second_rest + second_rows
    uppers = [second_x[0], second_rest[0], second_rows[2]]
    others = [second_x[1], second_rest[1], second_rows[0], second_rows[1], second_rows[3]]
    correlate(0, now)
    arrive(uppers)
    correlate(1, mid)

    share = depth // groups
    lane_part = lane_at // share
    for g in range(groups):
        for j in range(2):
            packed = None
            for x in range(cells_x):
                turn = (share * (x - g)) % depth
                piece = totals[j, x] if turn == 0 else pltpu.roll(totals[j, x], turn, 1)
                packed = piece if packed is None else jnp.where(lane_part == x, piece, packed)
            share_send[g, j] = packed
    third_round = [
        (remote(share_send.at[peers[d][0]], share_recv.at[d], peers[d]), True, True)
        for d in range(groups - 1)
    ]
    for copy, _, _ in third_round:
        copy.start()

    def put_out(f, c, x, value):
        adj_out[f, c, x] = value

    arrive(others)
    wall(1)
    for f in range(receivers):
        step(1, f, mid, now, put_out)

    for copy, _, _ in third_round:
        copy.wait_recv()
    scale_out = 1.0 / (STEPS * receivers * groups)
    for j in range(2):
        part = share_send[grp, j]
        for d in range(groups - 1):
            part = part + share_recv[d, j]
        part = part * scale_out
        for x in range(cells_x):
            piece = part if x == 0 else pltpu.roll(part, depth - share * x, 1)
            kern_out[j, x] = piece[:, 0:share]
    sent(first_x + first_moduli + first_rest + first_rows)
    sent(second_round)
    for copy, _, _ in third_round:
        copy.wait_send()


def hand_over(adj_made, kern_made, adj_out, kern_out, sems):
    adj_copy = pltpu.make_async_copy(adj_made, adj_out, sems.at[0])
    kern_copy = pltpu.make_async_copy(kern_made, kern_out, sems.at[1])
    adj_copy.start()
    kern_copy.start()
    adj_copy.wait()
    kern_copy.wait()


def local(
    fwd_now,
    fwd_prev,
    adj_now,
    adj_prev,
    lame_first,
    shear_mod,
    buoyancy,
    master_cell,
    master_lag,
    master_trace,
    receiver_cell,
    receiver_lag,
    receiver_trace,
):
    cells_x, cells_y, depth = lame_first.shape
    receivers = adj_now.shape[0]
    fields = receivers + 1
    sizes = tuple(lax.axis_size(axis) for axis in ("grp", "gx", "gy"))
    groups = sizes[0]
    lanes = -(-fields // 8) * 8
    block = (fields, 3, cells_x, cells_y, depth)
    scalar = pl.BlockSpec(memory_space=pltpu.SMEM)
    whole = pl.BlockSpec(memory_space=pltpu.HBM)
    vector = pl.BlockSpec(memory_space=pltpu.VMEM)

    def room(*shape):
        return pltpu.VMEM(shape, jnp.float32)

    def stay(value):
        return pltpu.with_memory_space_constraint(value, pltpu.HBM)

    made = pl.pallas_call(
        functools.partial(kernel, sizes),
        out_shape=(
            pltpu.VMEM(adj_now.shape, jnp.float32),
            pltpu.VMEM((2, cells_x, cells_y, depth // groups), jnp.float32),
        ),
        in_specs=[scalar] * 2 + [whole] * 11,
        out_specs=(vector, vector),
        scratch_shapes=[
            room(*block),
            room(*block),
            room(*block),
            room(cells_x + 1, cells_y, depth),
            room(cells_x + 1, cells_y, depth),
            room(cells_x, cells_y, depth),
            room(STEPS, fields, 3, cells_y, depth),
            room(STEPS, fields, 3, cells_y, depth),
            room(STEPS, 3, cells_x + 1, lanes, depth),
            room(STEPS, 3, cells_x + 1, lanes, depth),
            room(STEPS, 3, cells_x, lanes, depth),
            room(STEPS, 3, cells_x, lanes, depth),
            room(2 * cells_x, depth),
            room(2 * cells_x, depth),
            room(STEPS, 3, cells_x, lanes, depth),
            room(2, cells_x, cells_y, depth),
            room(groups, 2, cells_y, depth),
            room(groups - 1, 2, cells_y, depth),
            pltpu.SMEM((fields,), jnp.int32),
            pltpu.SMEM((fields * STEPS * 3,), jnp.float32),
            pltpu.SMEM((3,) + master_trace.shape[:1], jnp.float32),
            pltpu.SMEM((receivers,), jnp.int32),
            pltpu.SMEM((receivers,), jnp.int32),
            pltpu.SMEM((3,) + receiver_trace.shape[:2], jnp.float32),
            pltpu.SemaphoreType.DMA((11,)),
            pltpu.SemaphoreType.DMA((32,)),
            pltpu.SemaphoreType.DMA((32,)),
        ],
        compiler_params=pltpu.CompilerParams(
            collective_id=0, has_side_effects=True, vmem_limit_bytes=32 * 1024 * 1024
        ),
    )(
        master_cell,
        master_lag,
        stay(master_trace.T),
        stay(receiver_cell),
        stay(receiver_lag),
        stay(receiver_trace.transpose(2, 0, 1)),
        stay(fwd_now),
        stay(fwd_prev),
        stay(adj_now),
        stay(adj_prev),
        stay(lame_first),
        stay(shear_mod),
        stay(buoyancy),
    )
    made = [pltpu.with_memory_space_constraint(value, pltpu.VMEM) for value in made]
    return pl.pallas_call(
        hand_over,
        out_shape=tuple(jax.ShapeDtypeStruct(value.shape, value.dtype) for value in made),
        in_specs=[pl.BlockSpec(memory_space=pltpu.VMEM)] * 2,
        out_specs=(whole, whole),
        scratch_shapes=[pltpu.SemaphoreType.DMA((2,))],
    )(*made)


def solution(mesh):
    in_specs = (
        P(None, "gx", "gy", None),
        P(None, "gx", "gy", None),
        P("grp", None, "gx", "gy", None),
        P("grp", None, "gx", "gy", None),
        P("gx", "gy", None),
        P("gx", "gy", None),
        P("gx", "gy", None),
        P(),
        P(),
        P(),
        P("grp"),
        P("grp"),
        P("grp", None, None),
    )
    out_specs = (P("grp", None, "gx", "gy", None), P(None, "gx", "gy", "grp"))
    return jax.shard_map(local, mesh=mesh, in_specs=in_specs, out_specs=out_specs, check_vma=False)
```

```python
import functools

import jax
import jax.numpy as jnp
from jax import lax
from jax.experimental import pallas as pl
from jax.experimental.pallas import tpu as pltpu
from jax.sharding import PartitionSpec as P

STEPS = 2
MESH = pl.DeviceIdType.MESH

time_step_sq = 0.0625


def kernel(
    sizes,
    master_cell,
    master_lag,
    master_trace,
    receiver_cell,
    receiver_lag,
    receiver_trace,
    fwd_now,
    fwd_prev,
    adj_now,
    adj_prev,
    lame_first,
    shear_mod,
    buoyancy,
    adj_out,
    kern_out,
    now,
    prev,
    mid,
    lame,
    shear,
    buoy,
    xlo,
    xhi,
    ylo,
    yhi,
    row_first,
    row_last,
    mod_send,
    mod_recv,
    low_stress,
    totals,
    share_send,
    share_recv,
    cells,
    amps,
    master_trace_s,
    receiver_cell_s,
    receiver_lag_s,
    receiver_trace_s,
    load_sem,
    send_sem,
    recv_sem,
):
    groups, count_x, count_y = sizes
    receivers, _, cells_x, cells_y, depth = adj_now.shape
    fields = receivers + 1
    grp = lax.axis_index("grp")
    gx = lax.axis_index("gx")
    gy = lax.axis_index("gy")
    has_down = gx > 0
    has_up = gx < count_x - 1
    has_left = gy > 0
    has_right = gy < count_y - 1
    corner_ul = jnp.logical_and(has_up, has_left)
    corner_dr = jnp.logical_and(has_down, has_right)
    down = (grp, gx - 1, gy)
    up = (grp, gx + 1, gy)
    left = (grp, gx, gy - 1)
    right = (grp, gx, gy + 1)
    up_left = (grp, gx + 1, gy - 1)
    down_right = (grp, gx - 1, gy + 1)
    peers = [(lax.rem(grp + d, groups), gx, gy) for d in range(1, groups)]
    sides = (
        (has_down, down),
        (has_up, up),
        (has_left, left),
        (has_right, right),
        (corner_ul, up_left),
        (corner_dr, down_right),
    )

    barrier = pltpu.get_barrier_semaphore()
    expected = jnp.int32(groups - 1)
    for there, where in sides:
        expected = expected + there.astype(jnp.int32)

        @pl.when(there)
        def _():
            pl.semaphore_signal(barrier, inc=1, device_id=where, device_id_type=MESH)

    for where in peers:
        pl.semaphore_signal(barrier, inc=1, device_id=where, device_id_type=MESH)

    loads = [
        (adj_now, now.at[pl.ds(0, receivers)]),
        (fwd_now, now.at[receivers]),
        (lame_first, lame.at[pl.ds(1, cells_x)]),
        (shear_mod, shear.at[pl.ds(1, cells_x)]),
        (adj_prev, prev.at[pl.ds(0, receivers)]),
        (fwd_prev, prev.at[receivers]),
        (buoyancy, buoy),
        (master_trace, master_trace_s),
        (receiver_cell, receiver_cell_s),
        (receiver_lag, receiver_lag_s),
        (receiver_trace, receiver_trace_s),
    ]
    loads = [pltpu.make_async_copy(src, dst, load_sem.at[i]) for i, (src, dst) in enumerate(loads)]
    for copy in loads:
        copy.start()

    pl.semaphore_wait(barrier, expected)

    number = [0]

    def remote(src, dst, where):
        i = number[0]
        number[0] += 1
        return pltpu.make_async_remote_copy(
            src_ref=src,
            dst_ref=dst,
            send_sem=send_sem.at[i],
            recv_sem=recv_sem.at[i],
            device_id=where,
            device_id_type=MESH,
        )

    def rows(k):
        return [
            (remote(row_first.at[k, :, cells_x - 1], yhi.at[k, :, 0], up_left), corner_ul, corner_dr),
            (remote(row_last.at[k, :, 0], ylo.at[k, :, cells_x], down_right), corner_dr, corner_ul),
            (remote(row_first.at[k], yhi.at[k, :, pl.ds(1, cells_x)], left), has_left, has_right),
            (remote(row_last.at[k], ylo.at[k, :, pl.ds(0, cells_x)], right), has_right, has_left),
        ]

    def start(copies):
        for copy, sends, _ in copies:
            pl.when(sends)(copy.start)

    def arrive(copies):
        for copy, _, gets in copies:
            pl.when(gets)(copy.wait_recv)

    def sent(copies):
        for copy, sends, _ in copies:
            pl.when(sends)(copy.wait_send)

    last = cells_x - 1
    split = (receivers + 2) // 2
    group = pl.ds(0, split)
    rest = pl.ds(split, receivers - split)
    rest_all = pl.ds(split, fields - split)
    first_x = [
        (remote(adj_now.at[group, :, 0], xhi.at[0, group], down), has_down, has_up),
        (remote(adj_now.at[group, :, last], xlo.at[0, group], up), has_up, has_down),
    ]
    first_moduli = [
        (remote(lame_first.at[last], lame.at[0], up), has_up, has_down),
        (remote(shear_mod.at[last], shear.at[0], up), has_up, has_down),
        (remote(mod_send, mod_recv, right), has_right, has_left),
    ]
    first_rest = [
        (remote(adj_now.at[rest, :, 0], xhi.at[0, rest], down), has_down, has_up),
        (remote(adj_now.at[rest, :, last], xlo.at[0, rest], up), has_up, has_down),
        (remote(fwd_now.at[:, 0], xhi.at[0, receivers], down), has_down, has_up),
        (remote(fwd_now.at[:, last], xlo.at[0, receivers], up), has_up, has_down),
    ]
    first_rows = rows(0)
    start(first_moduli[:2])
    start(first_x)

    @pl.when(jnp.logical_not(has_down))
    def _():
        xlo[...] = jnp.zeros_like(xlo)
        lame[0] = jnp.zeros_like(lame[0])
        shear[0] = jnp.zeros_like(shear[0])

    @pl.when(jnp.logical_not(has_up))
    def _():
        xhi[...] = jnp.zeros_like(xhi)

    @pl.when(jnp.logical_not(has_left))
    def _():
        ylo[:, :, 0:cells_x] = jnp.zeros_like(ylo[:, :, 0:cells_x])
        mod_recv[...] = jnp.zeros_like(mod_recv)

    @pl.when(jnp.logical_not(has_right))
    def _():
        yhi[:, :, 1 : cells_x + 1] = jnp.zeros_like(yhi[:, :, 1 : cells_x + 1])

    @pl.when(jnp.logical_not(corner_ul))
    def _():
        ylo[:, :, cells_x] = jnp.zeros_like(ylo[:, :, cells_x])

    @pl.when(jnp.logical_not(corner_dr))
    def _():
        yhi[:, :, 0] = jnp.zeros_like(yhi[:, :, 0])

    row_first[...] = jnp.zeros_like(row_first)
    row_last[...] = jnp.zeros_like(row_last)

    for copy in loads[:4]:
        copy.wait()

    for f in range(fields):
        for c in range(3):
            for x in range(cells_x):
                row_first[0, c, x, f : f + 1, :] = now[f, c, x, 0:1, :]
                row_last[0, c, x, f : f + 1, :] = now[f, c, x, cells_y - 1 : cells_y, :]
    for x in range(cells_x):
        mod_send[x : x + 1] = lame[x + 1, cells_y - 1 : cells_y, :]
        mod_send[cells_x + x : cells_x + x + 1] = shear[x + 1, cells_y - 1 : cells_y, :]

    start(first_rows[2:])
    start(first_moduli[2:])
    start(first_rows[:2])
    start(first_rest)

    for copy in loads[4:]:
        copy.wait()

    for f in range(fields):
        master = f == receivers
        cells[f] = master_cell[0] if master else receiver_cell_s[f]
        lag = master_lag[0] if master else receiver_lag_s[f]
        for k in range(STEPS):
            for c in range(3):
                spot = (f * STEPS + k) * 3 + c
                amps[spot] = master_trace_s[c, lag + k] if master else receiver_trace_s[c, f, lag + k]

    row_at = lax.broadcasted_iota(jnp.int32, (cells_y, depth), 0)
    lane_at = lax.broadcasted_iota(jnp.int32, (cells_y, depth), 1)
    flat_at = row_at * depth + lane_at
    top = row_at == 0
    bottom = row_at == cells_y - 1
    front = lane_at == 0
    back = lane_at == depth - 1
    plane_cells = cells_y * count_y * depth
    first_cell = gx * cells_x * plane_cells + gy * cells_y * depth

    def next_z(v):
        return jnp.where(back, 0.0, pltpu.roll(v, depth - 1, 1))

    def last_z(v):
        return jnp.where(front, 0.0, pltpu.roll(v, 1, 1))

    def next_y(v, row):
        return jnp.where(bottom, row, pltpu.roll(v, cells_y - 1, 0))

    def last_y(v, row):
        return jnp.where(top, row, pltpu.roll(v, 1, 0))

    def wall(k):
        for x in range(cells_x):
            here = [ylo[k, c, x] for c in range(3)]
            beside = [ylo[k, c, x + 1] for c in range(3)]
            above = [row_first[k, c, x] for c in range(3)]
            lam = mod_recv[x : x + 1]
            mu = mod_recv[cells_x + x : cells_x + x + 1]
            grad_y = [above[c] - here[c] for c in range(3)]
            xy = grad_y[0] + (beside[1] - here[1])
            yz = (next_z(here[1]) - here[1]) + grad_y[2]
            dilation = (beside[0] - here[0]) + grad_y[1] + (next_z(here[2]) - here[2])
            low_stress[k, 0, x] = mu * xy
            low_stress[k, 1, x] = lam * dilation + 2.0 * mu * grad_y[1]
            low_stress[k, 2, x] = mu * yz

    def step(k, f, state, earlier, put):
        one = slice(f, f + 1)

        def row(c, x):
            return yhi[k, c, x + 1, one, :]

        here = [xlo[k, f, c] for c in range(3)]
        lam = lame[0]
        mu = shear[0]
        after = [state[f, c, 0] for c in range(3)]
        across = [next_y(here[c], row(c, -1)) for c in range(2)]
        along = [next_z(here[c]) for c in (0, 2)]
        xx = after[0] - here[0]
        dilation = xx + (across[1] - here[1]) + (along[1] - here[2])
        low = [
            lam * dilation + 2.0 * mu * xx,
            mu * ((across[0] - here[0]) + (after[1] - here[1])),
            mu * ((along[0] - here[0]) + (after[2] - here[2])),
        ]
        cell = cells[f]
        amp = [amps[(f * STEPS + k) * 3 + c] for c in range(3)]
        for x in range(cells_x):
            here = after
            after = [state[f, c, x + 1] if x < last else xhi[k, f, c] for c in range(3)]
            lam = lame[x + 1]
            mu = shear[x + 1]
            twice = 2.0 * mu
            gx_ = [after[c] - here[c] for c in range(3)]
            gy_ = [next_y(here[c], row(c, x)) - here[c] for c in range(3)]
            gz_ = [next_z(here[c]) - here[c] for c in range(3)]
            spread = lam * (gx_[0] + gy_[1] + gz_[2])
            xx = spread + twice * gx_[0]
            yy = spread + twice * gy_[1]
            zz = spread + twice * gz_[2]
            xy = mu * (gy_[0] + gx_[1])
            xz = mu * (gz_[0] + gx_[2])
            yz = mu * (gz_[1] + gy_[2])
            wall_xy, wall_yy, wall_yz = [low_stress[k, j, x, one, :] for j in range(3)]
            force = [
                (xx - low[0]) + (xy - last_y(xy, wall_xy)) + (xz - last_z(xz)),
                (xy - low[1]) + (yy - last_y(yy, wall_yy)) + (yz - last_z(yz)),
                (xz - low[2]) + (yz - last_y(yz, wall_yz)) + (zz - last_z(zz)),
            ]
            low = [xx, xy, xz]
            placed = flat_at == cell - (first_cell + x * plane_cells)
            scaled = time_step_sq * buoy[x]
            for c in range(3):
                moved = force[c] + jnp.where(placed, amp[c], 0.0)
                put(f, c, x, 2.0 * here[c] - earlier[f, c, x] + scaled * moved)

    def strain(planes, rows):
        for x in range(cells_x):
            here, after = planes[x], planes[x + 1]
            gx_ = [after[c] - here[c] for c in range(3)]
            gy_ = [next_y(here[c], rows[x][c]) - here[c] for c in range(3)]
            gz_ = [next_z(here[c]) - here[c] for c in range(3)]
            yield (
                gx_[0],
                gy_[1],
                gz_[2],
                gy_[0] + gx_[1],
                gz_[0] + gx_[2],
                gz_[1] + gy_[2],
            )

    def correlate(k, state):
        def summed(load):
            total = load(0)
            for f in range(1, receivers):
                total = total + load(f)
            return total

        whole, master = [], []
        for x in range(cells_x + 1):
            if x < cells_x:
                whole.append([summed(lambda f: state[f, c, x]) for c in range(3)])
                master.append([state[receivers, c, x] for c in range(3)])
            else:
                whole.append([summed(lambda f: xhi[k, f, c]) for c in range(3)])
                master.append([xhi[k, receivers, c] for c in range(3)])
        whole_rows = [
            [summed(lambda f: yhi[k, c, x + 1, f : f + 1, :]) for c in range(3)]
            for x in range(cells_x)
        ]
        master_rows = [
            [yhi[k, c, x + 1, receivers : receivers + 1, :] for c in range(3)]
            for x in range(cells_x)
        ]
        pairs = zip(strain(whole, whole_rows), strain(master, master_rows))
        for x, (a, b) in enumerate(pairs):
            swell = (a[0] + a[1] + a[2]) * (b[0] + b[1] + b[2])
            twist = 2.0 * (a[0] * b[0] + a[1] * b[1] + a[2] * b[2])
            twist = twist + (a[3] * b[3] + a[4] * b[4] + a[5] * b[5])
            if k == 0:
                totals[0, x] = swell
                totals[1, x] = twist
            else:
                totals[0, x] += swell
                totals[1, x] += twist

    arrive(first_moduli)
    arrive(first_rows)
    wall(0)
    arrive(first_x)

    def put_mid(f, c, x, value):
        mid[f, c, x] = value
        row_first[1, c, x, f : f + 1, :] = value[0:1]
        row_last[1, c, x, f : f + 1, :] = mid[f, c, x, cells_y - 1 : cells_y, :]

    for f in range(split):
        step(0, f, now, prev, put_mid)
    second_x = [
        (remote(mid.at[group, :, 0], xhi.at[1, group], down), has_down, has_up),
        (remote(mid.at[group, :, last], xlo.at[1, group], up), has_up, has_down),
    ]
    start(second_x)
    arrive(first_rest)
    for f in range(split, fields):
        step(0, f, now, prev, put_mid)
    second_rest = [
        (remote(mid.at[rest_all, :, 0], xhi.at[1, rest_all], down), has_down, has_up),
        (remote(mid.at[rest_all, :, last], xlo.at[1, rest_all], up), has_up, has_down),
    ]
    second_rows = rows(1)
    start(second_rows[2:])
    start(second_rest)
    start(second_rows[:2])
    second_round = second_x + second_rest + second_rows
    uppers = [second_x[0], second_rest[0], second_rows[2]]
    others = [second_x[1], second_rest[1], second_rows[0], second_rows[1], second_rows[3]]
    correlate(0, now)
    arrive(uppers)
    correlate(1, mid)

    share = depth // groups
    lane_part = lane_at // share
    for g in range(groups):
        for j in range(2):
            packed = None
            for x in range(cells_x):
                turn = (share * (x - g)) % depth
                piece = totals[j, x] if turn == 0 else pltpu.roll(totals[j, x], turn, 1)
                packed = piece if packed is None else jnp.where(lane_part == x, piece, packed)
            share_send[g, j] = packed
    third_round = [
        (remote(share_send.at[peers[d][0]], share_recv.at[d], peers[d]), True, True)
        for d in range(groups - 1)
    ]
    for copy, _, _ in third_round:
        copy.start()

    def put_out(f, c, x, value):
        adj_out[f, c, x] = value

    arrive(others)
    wall(1)
    for f in range(receivers):
        step(1, f, mid, now, put_out)

    for copy, _, _ in third_round:
        copy.wait_recv()
    scale_out = 1.0 / (STEPS * receivers * groups)
    for j in range(2):
        part = share_send[grp, j]
        for d in range(groups - 1):
            part = part + share_recv[d, j]
        part = part * scale_out
        for x in range(cells_x):
            piece = part if x == 0 else pltpu.roll(part, depth - share * x, 1)
            kern_out[j, x] = piece[:, 0:share]
    sent(first_x + first_moduli + first_rest + first_rows)
    sent(second_round)
    for copy, _, _ in third_round:
        copy.wait_send()


def hand_over(adj_made, kern_made, adj_out, kern_out, sems):
    adj_copy = pltpu.make_async_copy(adj_made, adj_out, sems.at[0])
    kern_copy = pltpu.make_async_copy(kern_made, kern_out, sems.at[1])
    adj_copy.start()
    kern_copy.start()
    adj_copy.wait()
    kern_copy.wait()


def local(
    fwd_now,
    fwd_prev,
    adj_now,
    adj_prev,
    lame_first,
    shear_mod,
    buoyancy,
    master_cell,
    master_lag,
    master_trace,
    receiver_cell,
    receiver_lag,
    receiver_trace,
):
    cells_x, cells_y, depth = lame_first.shape
    receivers = adj_now.shape[0]
    fields = receivers + 1
    sizes = tuple(lax.axis_size(axis) for axis in ("grp", "gx", "gy"))
    groups = sizes[0]
    lanes = -(-fields // 8) * 8
    block = (fields, 3, cells_x, cells_y, depth)
    scalar = pl.BlockSpec(memory_space=pltpu.SMEM)
    whole = pl.BlockSpec(memory_space=pltpu.HBM)
    vector = pl.BlockSpec(memory_space=pltpu.VMEM)

    def room(*shape):
        return pltpu.VMEM(shape, jnp.float32)

    def stay(value):
        return pltpu.with_memory_space_constraint(value, pltpu.HBM)

    made = pl.pallas_call(
        functools.partial(kernel, sizes),
        out_shape=(
            pltpu.VMEM(adj_now.shape, jnp.float32),
            pltpu.VMEM((2, cells_x, cells_y, depth // groups), jnp.float32),
        ),
        in_specs=[scalar] * 2 + [whole] * 11,
        out_specs=(vector, vector),
        scratch_shapes=[
            room(*block),
            room(*block),
            room(*block),
            room(cells_x + 1, cells_y, depth),
            room(cells_x + 1, cells_y, depth),
            room(cells_x, cells_y, depth),
            room(STEPS, fields, 3, cells_y, depth),
            room(STEPS, fields, 3, cells_y, depth),
            room(STEPS, 3, cells_x + 1, lanes, depth),
            room(STEPS, 3, cells_x + 1, lanes, depth),
            room(STEPS, 3, cells_x, lanes, depth),
            room(STEPS, 3, cells_x, lanes, depth),
            room(2 * cells_x, depth),
            room(2 * cells_x, depth),
            room(STEPS, 3, cells_x, lanes, depth),
            room(2, cells_x, cells_y, depth),
            room(groups, 2, cells_y, depth),
            room(groups - 1, 2, cells_y, depth),
            pltpu.SMEM((fields,), jnp.int32),
            pltpu.SMEM((fields * STEPS * 3,), jnp.float32),
            pltpu.SMEM((3,) + master_trace.shape[:1], jnp.float32),
            pltpu.SMEM((receivers,), jnp.int32),
            pltpu.SMEM((receivers,), jnp.int32),
            pltpu.SMEM((3,) + receiver_trace.shape[:2], jnp.float32),
            pltpu.SemaphoreType.DMA((11,)),
            pltpu.SemaphoreType.DMA((32,)),
            pltpu.SemaphoreType.DMA((32,)),
        ],
        compiler_params=pltpu.CompilerParams(
            collective_id=0, has_side_effects=True, vmem_limit_bytes=32 * 1024 * 1024
        ),
    )(
        master_cell,
        master_lag,
        stay(master_trace.T),
        stay(receiver_cell),
        stay(receiver_lag),
        stay(receiver_trace.transpose(2, 0, 1)),
        stay(fwd_now),
        stay(fwd_prev),
        stay(adj_now),
        stay(adj_prev),
        stay(lame_first),
        stay(shear_mod),
        stay(buoyancy),
    )
    made = [pltpu.with_memory_space_constraint(value, pltpu.VMEM) for value in made]
    return pl.pallas_call(
        hand_over,
        out_shape=tuple(jax.ShapeDtypeStruct(value.shape, value.dtype) for value in made),
        in_specs=[pl.BlockSpec(memory_space=pltpu.VMEM)] * 2,
        out_specs=(whole, whole),
        scratch_shapes=[pltpu.SemaphoreType.DMA((2,))],
    )(*made)


def solution(mesh):
    in_specs = (
        P(None, "gx", "gy", None),
        P(None, "gx", "gy", None),
        P("grp", None, "gx", "gy", None),
        P("grp", None, "gx", "gy", None),
        P("gx", "gy", None),
        P("gx", "gy", None),
        P("gx", "gy", None),
        P(),
        P(),
        P(),
        P("grp"),
        P("grp"),
        P("grp", None, None),
    )
    out_specs = (P("grp", None, "gx", "gy", None), P(None, "gx", "gy", "grp"))
    return jax.shard_map(local, mesh=mesh, in_specs=in_specs, out_specs=out_specs, check_vma=False)
```

```python
import functools

import jax
import jax.numpy as jnp
from jax import lax
from jax.experimental import pallas as pl
from jax.experimental.pallas import tpu as pltpu
from jax.sharding import PartitionSpec as P

STEPS = 2
MESH = pl.DeviceIdType.MESH

time_step_sq = 0.0625


def kernel(
    sizes,
    master_cell,
    master_lag,
    master_trace,
    receiver_cell,
    receiver_lag,
    receiver_trace,
    fwd_now,
    fwd_prev,
    adj_now,
    adj_prev,
    lame_first,
    shear_mod,
    buoyancy,
    adj_out,
    kern_out,
    now,
    prev,
    mid,
    lame,
    shear,
    buoy,
    xlo,
    xhi,
    ylo,
    yhi,
    row_first,
    row_last,
    mod_send,
    mod_recv,
    low_stress,
    totals,
    share_send,
    share_recv,
    cells,
    amps,
    master_trace_s,
    receiver_cell_s,
    receiver_lag_s,
    receiver_trace_s,
    load_sem,
    send_sem,
    recv_sem,
):
    groups, count_x, count_y = sizes
    receivers, _, cells_x, cells_y, depth = adj_now.shape
    fields = receivers + 1
    grp = lax.axis_index("grp")
    gx = lax.axis_index("gx")
    gy = lax.axis_index("gy")
    has_down = gx > 0
    has_up = gx < count_x - 1
    has_left = gy > 0
    has_right = gy < count_y - 1
    corner_ul = jnp.logical_and(has_up, has_left)
    corner_dr = jnp.logical_and(has_down, has_right)
    down = (grp, gx - 1, gy)
    up = (grp, gx + 1, gy)
    left = (grp, gx, gy - 1)
    right = (grp, gx, gy + 1)
    up_left = (grp, gx + 1, gy - 1)
    down_right = (grp, gx - 1, gy + 1)
    peers = [(lax.rem(grp + d, groups), gx, gy) for d in range(1, groups)]
    sides = (
        (has_down, down),
        (has_up, up),
        (has_left, left),
        (has_right, right),
        (corner_ul, up_left),
        (corner_dr, down_right),
    )

    barrier = pltpu.get_barrier_semaphore()
    expected = jnp.int32(groups - 1)
    for there, where in sides:
        expected = expected + there.astype(jnp.int32)

        @pl.when(there)
        def _():
            pl.semaphore_signal(barrier, inc=1, device_id=where, device_id_type=MESH)

    for where in peers:
        pl.semaphore_signal(barrier, inc=1, device_id=where, device_id_type=MESH)

    loads = [
        (adj_now, now.at[pl.ds(0, receivers)]),
        (fwd_now, now.at[receivers]),
        (lame_first, lame.at[pl.ds(1, cells_x)]),
        (shear_mod, shear.at[pl.ds(1, cells_x)]),
        (adj_prev, prev.at[pl.ds(0, receivers)]),
        (fwd_prev, prev.at[receivers]),
        (buoyancy, buoy),
        (master_trace, master_trace_s),
        (receiver_cell, receiver_cell_s),
        (receiver_lag, receiver_lag_s),
        (receiver_trace, receiver_trace_s),
    ]
    loads = [pltpu.make_async_copy(src, dst, load_sem.at[i]) for i, (src, dst) in enumerate(loads)]
    for copy in loads:
        copy.start()

    pl.semaphore_wait(barrier, expected)

    number = [0]

    def remote(src, dst, where):
        i = number[0]
        number[0] += 1
        return pltpu.make_async_remote_copy(
            src_ref=src,
            dst_ref=dst,
            send_sem=send_sem.at[i],
            recv_sem=recv_sem.at[i],
            device_id=where,
            device_id_type=MESH,
        )

    def rows(k):
        return [
            (remote(row_first.at[k, :, cells_x - 1], yhi.at[k, :, 0], up_left), corner_ul, corner_dr),
            (remote(row_last.at[k, :, 0], ylo.at[k, :, cells_x], down_right), corner_dr, corner_ul),
            (remote(row_first.at[k], yhi.at[k, :, pl.ds(1, cells_x)], left), has_left, has_right),
            (remote(row_last.at[k], ylo.at[k, :, pl.ds(0, cells_x)], right), has_right, has_left),
        ]

    def start(copies):
        for copy, sends, _ in copies:
            pl.when(sends)(copy.start)

    def arrive(copies):
        for copy, _, gets in copies:
            pl.when(gets)(copy.wait_recv)

    def sent(copies):
        for copy, sends, _ in copies:
            pl.when(sends)(copy.wait_send)

    last = cells_x - 1
    split = (receivers + 2) // 2
    group = pl.ds(0, split)
    rest = pl.ds(split, receivers - split)
    rest_all = pl.ds(split, fields - split)
    first_x = [
        (remote(adj_now.at[group, :, 0], xhi.at[0, group], down), has_down, has_up),
        (remote(adj_now.at[group, :, last], xlo.at[0, group], up), has_up, has_down),
    ]
    first_moduli = [
        (remote(lame_first.at[last], lame.at[0], up), has_up, has_down),
        (remote(shear_mod.at[last], shear.at[0], up), has_up, has_down),
        (remote(mod_send, mod_recv, right), has_right, has_left),
    ]
    first_rest = [
        (remote(adj_now.at[rest, :, 0], xhi.at[0, rest], down), has_down, has_up),
        (remote(adj_now.at[rest, :, last], xlo.at[0, rest], up), has_up, has_down),
        (remote(fwd_now.at[:, 0], xhi.at[0, receivers], down), has_down, has_up),
        (remote(fwd_now.at[:, last], xlo.at[0, receivers], up), has_up, has_down),
    ]
    first_rows = rows(0)
    start(first_moduli[:2])
    start(first_x)

    @pl.when(jnp.logical_not(has_down))
    def _():
        xlo[...] = jnp.zeros_like(xlo)
        lame[0] = jnp.zeros_like(lame[0])
        shear[0] = jnp.zeros_like(shear[0])

    @pl.when(jnp.logical_not(has_up))
    def _():
        xhi[...] = jnp.zeros_like(xhi)

    @pl.when(jnp.logical_not(has_left))
    def _():
        ylo[:, :, 0:cells_x] = jnp.zeros_like(ylo[:, :, 0:cells_x])
        mod_recv[...] = jnp.zeros_like(mod_recv)

    @pl.when(jnp.logical_not(has_right))
    def _():
        yhi[:, :, 1 : cells_x + 1] = jnp.zeros_like(yhi[:, :, 1 : cells_x + 1])

    @pl.when(jnp.logical_not(corner_ul))
    def _():
        ylo[:, :, cells_x] = jnp.zeros_like(ylo[:, :, cells_x])

    @pl.when(jnp.logical_not(corner_dr))
    def _():
        yhi[:, :, 0] = jnp.zeros_like(yhi[:, :, 0])

    row_first[...] = jnp.zeros_like(row_first)
    row_last[...] = jnp.zeros_like(row_last)

    for copy in loads[:4]:
        copy.wait()

    for f in range(fields):
        for c in range(3):
            for x in range(cells_x):
                row_first[0, c, x, f : f + 1, :] = now[f, c, x, 0:1, :]
                row_last[0, c, x, f : f + 1, :] = now[f, c, x, cells_y - 1 : cells_y, :]
    for x in range(cells_x):
        mod_send[x : x + 1] = lame[x + 1, cells_y - 1 : cells_y, :]
        mod_send[cells_x + x : cells_x + x + 1] = shear[x + 1, cells_y - 1 : cells_y, :]

    start(first_rows[2:])
    start(first_moduli[2:])
    start(first_rows[:2])
    start(first_rest)

    for copy in loads[4:]:
        copy.wait()

    for f in range(fields):
        master = f == receivers
        cells[f] = master_cell[0] if master else receiver_cell_s[f]
        lag = master_lag[0] if master else receiver_lag_s[f]
        for k in range(STEPS):
            for c in range(3):
                spot = (f * STEPS + k) * 3 + c
                amps[spot] = master_trace_s[c, lag + k] if master else receiver_trace_s[c, f, lag + k]

    row_at = lax.broadcasted_iota(jnp.int32, (cells_y, depth), 0)
    lane_at = lax.broadcasted_iota(jnp.int32, (cells_y, depth), 1)
    flat_at = row_at * depth + lane_at
    top = row_at == 0
    bottom = row_at == cells_y - 1
    front = lane_at == 0
    back = lane_at == depth - 1
    plane_cells = cells_y * count_y * depth
    first_cell = gx * cells_x * plane_cells + gy * cells_y * depth

    def next_z(v):
        return jnp.where(back, 0.0, pltpu.roll(v, depth - 1, 1))

    def last_z(v):
        return jnp.where(front, 0.0, pltpu.roll(v, 1, 1))

    def next_y(v, row):
        return jnp.where(bottom, row, pltpu.roll(v, cells_y - 1, 0))

    def last_y(v, row):
        return jnp.where(top, row, pltpu.roll(v, 1, 0))

    def wall(k):
        for x in range(cells_x):
            here = [ylo[k, c, x] for c in range(3)]
            beside = [ylo[k, c, x + 1] for c in range(3)]
            above = [row_first[k, c, x] for c in range(3)]
            lam = mod_recv[x : x + 1]
            mu = mod_recv[cells_x + x : cells_x + x + 1]
            grad_y = [above[c] - here[c] for c in range(3)]
            xy = grad_y[0] + (beside[1] - here[1])
            yz = (next_z(here[1]) - here[1]) + grad_y[2]
            dilation = (beside[0] - here[0]) + grad_y[1] + (next_z(here[2]) - here[2])
            low_stress[k, 0, x] = mu * xy
            low_stress[k, 1, x] = lam * dilation + 2.0 * mu * grad_y[1]
            low_stress[k, 2, x] = mu * yz

    def step(k, f, state, earlier, put):
        one = slice(f, f + 1)

        def row(c, x):
            return yhi[k, c, x + 1, one, :]

        here = [xlo[k, f, c] for c in range(3)]
        lam = lame[0]
        mu = shear[0]
        after = [state[f, c, 0] for c in range(3)]
        across = [next_y(here[c], row(c, -1)) for c in range(2)]
        along = [next_z(here[c]) for c in (0, 2)]
        xx = after[0] - here[0]
        dilation = xx + (across[1] - here[1]) + (along[1] - here[2])
        low = [
            lam * dilation + 2.0 * mu * xx,
            mu * ((across[0] - here[0]) + (after[1] - here[1])),
            mu * ((along[0] - here[0]) + (after[2] - here[2])),
        ]
        cell = cells[f]
        amp = [amps[(f * STEPS + k) * 3 + c] for c in range(3)]
        for x in range(cells_x):
            here = after
            after = [state[f, c, x + 1] if x < last else xhi[k, f, c] for c in range(3)]
            lam = lame[x + 1]
            mu = shear[x + 1]
            twice = 2.0 * mu
            gx_ = [after[c] - here[c] for c in range(3)]
            gy_ = [next_y(here[c], row(c, x)) - here[c] for c in range(3)]
            gz_ = [next_z(here[c]) - here[c] for c in range(3)]
            spread = lam * (gx_[0] + gy_[1] + gz_[2])
            xx = spread + twice * gx_[0]
            yy = spread + twice * gy_[1]
            zz = spread + twice * gz_[2]
            xy = mu * (gy_[0] + gx_[1])
            xz = mu * (gz_[0] + gx_[2])
            yz = mu * (gz_[1] + gy_[2])
            wall_xy, wall_yy, wall_yz = [low_stress[k, j, x, one, :] for j in range(3)]
            force = [
                (xx - low[0]) + (xy - last_y(xy, wall_xy)) + (xz - last_z(xz)),
                (xy - low[1]) + (yy - last_y(yy, wall_yy)) + (yz - last_z(yz)),
                (xz - low[2]) + (yz - last_y(yz, wall_yz)) + (zz - last_z(zz)),
            ]
            low = [xx, xy, xz]
            placed = flat_at == cell - (first_cell + x * plane_cells)
            scaled = time_step_sq * buoy[x]
            for c in range(3):
                moved = force[c] + jnp.where(placed, amp[c], 0.0)
                put(f, c, x, 2.0 * here[c] - earlier[f, c, x] + scaled * moved)

    def prepare(planes):
        along = [[next_z(v) - v for v in plane] for plane in planes]
        turned = [[pltpu.roll(v, cells_y - 1, 0) for v in plane] for plane in planes]
        return planes, along, turned

    def strain(prepared, far, rows):
        planes, along, turned = prepared
        for x in range(cells_x):
            here = planes[x]
            after = planes[x + 1] if x < last else far
            gx_ = [after[c] - here[c] for c in range(3)]
            gy_ = [jnp.where(bottom, rows[x][c], turned[x][c]) - here[c] for c in range(3)]
            gz_ = along[x]
            yield (
                gx_[0],
                gy_[1],
                gz_[2],
                gy_[0] + gx_[1],
                gz_[0] + gx_[2],
                gz_[1] + gy_[2],
            )

    def summed(load):
        total = load(0)
        for f in range(1, receivers):
            total = total + load(f)
        return total

    def blocks(state):
        whole = [
            [summed(lambda f: state[f, c, x]) for c in range(3)] for x in range(cells_x)
        ]
        master = [[state[receivers, c, x] for c in range(3)] for x in range(cells_x)]
        return prepare(whole), prepare(master)

    def correlate(k, whole, master):
        whole_far = [summed(lambda f: xhi[k, f, c]) for c in range(3)]
        master_far = [xhi[k, receivers, c] for c in range(3)]
        whole_rows = [
            [summed(lambda f: yhi[k, c, x + 1, f : f + 1, :]) for c in range(3)]
            for x in range(cells_x)
        ]
        master_rows = [
            [yhi[k, c, x + 1, receivers : receivers + 1, :] for c in range(3)]
            for x in range(cells_x)
        ]
        pairs = zip(
            strain(whole, whole_far, whole_rows), strain(master, master_far, master_rows)
        )
        for x, (a, b) in enumerate(pairs):
            swell = (a[0] + a[1] + a[2]) * (b[0] + b[1] + b[2])
            twist = 2.0 * (a[0] * b[0] + a[1] * b[1] + a[2] * b[2])
            twist = twist + (a[3] * b[3] + a[4] * b[4] + a[5] * b[5])
            if k == 0:
                totals[0, x] = swell
                totals[1, x] = twist
            else:
                totals[0, x] += swell
                totals[1, x] += twist

    arrive(first_moduli)
    arrive(first_rows)
    wall(0)
    arrive(first_x)

    def put_mid(f, c, x, value):
        mid[f, c, x] = value
        row_first[1, c, x, f : f + 1, :] = value[0:1]
        row_last[1, c, x, f : f + 1, :] = mid[f, c, x, cells_y - 1 : cells_y, :]

    for f in range(split):
        step(0, f, now, prev, put_mid)
    second_x = [
        (remote(mid.at[group, :, 0], xhi.at[1, group], down), has_down, has_up),
        (remote(mid.at[group, :, last], xlo.at[1, group], up), has_up, has_down),
    ]
    start(second_x)
    arrive(first_rest)
    for f in range(split, fields):
        step(0, f, now, prev, put_mid)
    second_rest = [
        (remote(mid.at[rest_all, :, 0], xhi.at[1, rest_all], down), has_down, has_up),
        (remote(mid.at[rest_all, :, last], xlo.at[1, rest_all], up), has_up, has_down),
    ]
    second_rows = rows(1)
    start(second_rows[2:])
    start(second_rest)
    start(second_rows[:2])
    second_round = second_x + second_rest + second_rows
    uppers = [second_x[0], second_rest[0], second_rows[2]]
    others = [second_x[1], second_rest[1], second_rows[0], second_rows[1], second_rows[3]]
    correlate(0, *blocks(now))
    ready = blocks(mid)
    arrive(uppers)
    correlate(1, *ready)

    share = depth // groups
    lane_part = lane_at // share
    for g in range(groups):
        for j in range(2):
            packed = None
            for x in range(cells_x):
                turn = (share * (x - g)) % depth
                piece = totals[j, x] if turn == 0 else pltpu.roll(totals[j, x], turn, 1)
                packed = piece if packed is None else jnp.where(lane_part == x, piece, packed)
            share_send[g, j] = packed
    third_round = [
        (remote(share_send.at[peers[d][0]], share_recv.at[d], peers[d]), True, True)
        for d in range(groups - 1)
    ]
    for copy, _, _ in third_round:
        copy.start()

    def put_out(f, c, x, value):
        adj_out[f, c, x] = value

    arrive(others)
    wall(1)
    for f in range(receivers):
        step(1, f, mid, now, put_out)

    for copy, _, _ in third_round:
        copy.wait_recv()
    scale_out = 1.0 / (STEPS * receivers * groups)
    for j in range(2):
        part = share_send[grp, j]
        for d in range(groups - 1):
            part = part + share_recv[d, j]
        part = part * scale_out
        for x in range(cells_x):
            piece = part if x == 0 else pltpu.roll(part, depth - share * x, 1)
            kern_out[j, x] = piece[:, 0:share]
    sent(first_x + first_moduli + first_rest + first_rows)
    sent(second_round)
    for copy, _, _ in third_round:
        copy.wait_send()


def hand_over(adj_made, kern_made, adj_out, kern_out, sems):
    adj_copy = pltpu.make_async_copy(adj_made, adj_out, sems.at[0])
    kern_copy = pltpu.make_async_copy(kern_made, kern_out, sems.at[1])
    adj_copy.start()
    kern_copy.start()
    adj_copy.wait()
    kern_copy.wait()


def local(
    fwd_now,
    fwd_prev,
    adj_now,
    adj_prev,
    lame_first,
    shear_mod,
    buoyancy,
    master_cell,
    master_lag,
    master_trace,
    receiver_cell,
    receiver_lag,
    receiver_trace,
):
    cells_x, cells_y, depth = lame_first.shape
    receivers = adj_now.shape[0]
    fields = receivers + 1
    sizes = tuple(lax.axis_size(axis) for axis in ("grp", "gx", "gy"))
    groups = sizes[0]
    lanes = -(-fields // 8) * 8
    block = (fields, 3, cells_x, cells_y, depth)
    scalar = pl.BlockSpec(memory_space=pltpu.SMEM)
    whole = pl.BlockSpec(memory_space=pltpu.HBM)
    vector = pl.BlockSpec(memory_space=pltpu.VMEM)

    def room(*shape):
        return pltpu.VMEM(shape, jnp.float32)

    def stay(value):
        return pltpu.with_memory_space_constraint(value, pltpu.HBM)

    made = pl.pallas_call(
        functools.partial(kernel, sizes),
        out_shape=(
            pltpu.VMEM(adj_now.shape, jnp.float32),
            pltpu.VMEM((2, cells_x, cells_y, depth // groups), jnp.float32),
        ),
        in_specs=[scalar] * 2 + [whole] * 11,
        out_specs=(vector, vector),
        scratch_shapes=[
            room(*block),
            room(*block),
            room(*block),
            room(cells_x + 1, cells_y, depth),
            room(cells_x + 1, cells_y, depth),
            room(cells_x, cells_y, depth),
            room(STEPS, fields, 3, cells_y, depth),
            room(STEPS, fields, 3, cells_y, depth),
            room(STEPS, 3, cells_x + 1, lanes, depth),
            room(STEPS, 3, cells_x + 1, lanes, depth),
            room(STEPS, 3, cells_x, lanes, depth),
            room(STEPS, 3, cells_x, lanes, depth),
            room(2 * cells_x, depth),
            room(2 * cells_x, depth),
            room(STEPS, 3, cells_x, lanes, depth),
            room(2, cells_x, cells_y, depth),
            room(groups, 2, cells_y, depth),
            room(groups - 1, 2, cells_y, depth),
            pltpu.SMEM((fields,), jnp.int32),
            pltpu.SMEM((fields * STEPS * 3,), jnp.float32),
            pltpu.SMEM((3,) + master_trace.shape[:1], jnp.float32),
            pltpu.SMEM((receivers,), jnp.int32),
            pltpu.SMEM((receivers,), jnp.int32),
            pltpu.SMEM((3,) + receiver_trace.shape[:2], jnp.float32),
            pltpu.SemaphoreType.DMA((11,)),
            pltpu.SemaphoreType.DMA((32,)),
            pltpu.SemaphoreType.DMA((32,)),
        ],
        compiler_params=pltpu.CompilerParams(
            collective_id=0, has_side_effects=True, vmem_limit_bytes=32 * 1024 * 1024
        ),
    )(
        master_cell,
        master_lag,
        stay(master_trace.T),
        stay(receiver_cell),
        stay(receiver_lag),
        stay(receiver_trace.transpose(2, 0, 1)),
        stay(fwd_now),
        stay(fwd_prev),
        stay(adj_now),
        stay(adj_prev),
        stay(lame_first),
        stay(shear_mod),
        stay(buoyancy),
    )
    made = [pltpu.with_memory_space_constraint(value, pltpu.VMEM) for value in made]
    return pl.pallas_call(
        hand_over,
        out_shape=tuple(jax.ShapeDtypeStruct(value.shape, value.dtype) for value in made),
        in_specs=[pl.BlockSpec(memory_space=pltpu.VMEM)] * 2,
        out_specs=(whole, whole),
        scratch_shapes=[pltpu.SemaphoreType.DMA((2,))],
    )(*made)


def solution(mesh):
    in_specs = (
        P(None, "gx", "gy", None),
        P(None, "gx", "gy", None),
        P("grp", None, "gx", "gy", None),
        P("grp", None, "gx", "gy", None),
        P("gx", "gy", None),
        P("gx", "gy", None),
        P("gx", "gy", None),
        P(),
        P(),
        P(),
        P("grp"),
        P("grp"),
        P("grp", None, None),
    )
    out_specs = (P("grp", None, "gx", "gy", None), P(None, "gx", "gy", "grp"))
    return jax.shard_map(local, mesh=mesh, in_specs=in_specs, out_specs=out_specs, check_vma=False)
```

```python
import functools

import jax
import jax.numpy as jnp
from jax import lax
from jax.experimental import pallas as pl
from jax.experimental.pallas import tpu as pltpu
from jax.sharding import PartitionSpec as P

STEPS = 2
MESH = pl.DeviceIdType.MESH

time_step_sq = 0.0625


def kernel(
    sizes,
    master_cell,
    master_lag,
    master_trace,
    receiver_cell,
    receiver_lag,
    receiver_trace,
    fwd_now,
    fwd_prev,
    adj_now,
    adj_prev,
    lame_first,
    shear_mod,
    buoyancy,
    adj_out,
    kern_out,
    now,
    prev,
    mid,
    lame,
    shear,
    buoy,
    xlo,
    xhi,
    ylo,
    yhi,
    row_first,
    row_last,
    mod_send,
    mod_recv,
    low_stress,
    turned_now,
    along_now,
    totals,
    share_send,
    share_recv,
    cells,
    amps,
    master_trace_s,
    receiver_cell_s,
    receiver_lag_s,
    receiver_trace_s,
    load_sem,
    send_sem,
    recv_sem,
):
    groups, count_x, count_y = sizes
    receivers, _, cells_x, cells_y, depth = adj_now.shape
    fields = receivers + 1
    grp = lax.axis_index("grp")
    gx = lax.axis_index("gx")
    gy = lax.axis_index("gy")
    has_down = gx > 0
    has_up = gx < count_x - 1
    has_left = gy > 0
    has_right = gy < count_y - 1
    corner_ul = jnp.logical_and(has_up, has_left)
    corner_dr = jnp.logical_and(has_down, has_right)
    down = (grp, gx - 1, gy)
    up = (grp, gx + 1, gy)
    left = (grp, gx, gy - 1)
    right = (grp, gx, gy + 1)
    up_left = (grp, gx + 1, gy - 1)
    down_right = (grp, gx - 1, gy + 1)
    peers = [(lax.rem(grp + d, groups), gx, gy) for d in range(1, groups)]
    sides = (
        (has_down, down),
        (has_up, up),
        (has_left, left),
        (has_right, right),
        (corner_ul, up_left),
        (corner_dr, down_right),
    )

    barrier = pltpu.get_barrier_semaphore()
    expected = jnp.int32(groups - 1)
    for there, where in sides:
        expected = expected + there.astype(jnp.int32)

        @pl.when(there)
        def _():
            pl.semaphore_signal(barrier, inc=1, device_id=where, device_id_type=MESH)

    for where in peers:
        pl.semaphore_signal(barrier, inc=1, device_id=where, device_id_type=MESH)

    loads = [
        (adj_now, now.at[pl.ds(0, receivers)]),
        (fwd_now, now.at[receivers]),
        (lame_first, lame.at[pl.ds(1, cells_x)]),
        (shear_mod, shear.at[pl.ds(1, cells_x)]),
        (adj_prev, prev.at[pl.ds(0, receivers)]),
        (fwd_prev, prev.at[receivers]),
        (buoyancy, buoy),
        (master_trace, master_trace_s),
        (receiver_cell, receiver_cell_s),
        (receiver_lag, receiver_lag_s),
        (receiver_trace, receiver_trace_s),
    ]
    loads = [pltpu.make_async_copy(src, dst, load_sem.at[i]) for i, (src, dst) in enumerate(loads)]
    for copy in loads:
        copy.start()

    pl.semaphore_wait(barrier, expected)

    number = [0]

    def remote(src, dst, where):
        i = number[0]
        number[0] += 1
        return pltpu.make_async_remote_copy(
            src_ref=src,
            dst_ref=dst,
            send_sem=send_sem.at[i],
            recv_sem=recv_sem.at[i],
            device_id=where,
            device_id_type=MESH,
        )

    def rows(k):
        return [
            (remote(row_first.at[k, :, cells_x - 1], yhi.at[k, :, 0], up_left), corner_ul, corner_dr),
            (remote(row_last.at[k, :, 0], ylo.at[k, :, cells_x], down_right), corner_dr, corner_ul),
            (remote(row_first.at[k], yhi.at[k, :, pl.ds(1, cells_x)], left), has_left, has_right),
            (remote(row_last.at[k], ylo.at[k, :, pl.ds(0, cells_x)], right), has_right, has_left),
        ]

    def start(copies):
        for copy, sends, _ in copies:
            pl.when(sends)(copy.start)

    def arrive(copies):
        for copy, _, gets in copies:
            pl.when(gets)(copy.wait_recv)

    def sent(copies):
        for copy, sends, _ in copies:
            pl.when(sends)(copy.wait_send)

    last = cells_x - 1
    split = (receivers + 2) // 2
    group = pl.ds(0, split)
    rest = pl.ds(split, receivers - split)
    rest_all = pl.ds(split, fields - split)
    first_x = [
        (remote(adj_now.at[group, :, 0], xhi.at[0, group], down), has_down, has_up),
        (remote(adj_now.at[group, :, last], xlo.at[0, group], up), has_up, has_down),
    ]
    first_moduli = [
        (remote(lame_first.at[last], lame.at[0], up), has_up, has_down),
        (remote(shear_mod.at[last], shear.at[0], up), has_up, has_down),
        (remote(mod_send, mod_recv, right), has_right, has_left),
    ]
    first_rest = [
        (remote(adj_now.at[rest, :, 0], xhi.at[0, rest], down), has_down, has_up),
        (remote(adj_now.at[rest, :, last], xlo.at[0, rest], up), has_up, has_down),
        (remote(fwd_now.at[:, 0], xhi.at[0, receivers], down), has_down, has_up),
        (remote(fwd_now.at[:, last], xlo.at[0, receivers], up), has_up, has_down),
    ]
    first_rows = rows(0)
    start(first_moduli[:2])
    start(first_x)

    @pl.when(jnp.logical_not(has_down))
    def _():
        xlo[...] = jnp.zeros_like(xlo)
        lame[0] = jnp.zeros_like(lame[0])
        shear[0] = jnp.zeros_like(shear[0])

    @pl.when(jnp.logical_not(has_up))
    def _():
        xhi[...] = jnp.zeros_like(xhi)

    @pl.when(jnp.logical_not(has_left))
    def _():
        ylo[:, :, 0:cells_x] = jnp.zeros_like(ylo[:, :, 0:cells_x])
        mod_recv[...] = jnp.zeros_like(mod_recv)

    @pl.when(jnp.logical_not(has_right))
    def _():
        yhi[:, :, 1 : cells_x + 1] = jnp.zeros_like(yhi[:, :, 1 : cells_x + 1])

    @pl.when(jnp.logical_not(corner_ul))
    def _():
        ylo[:, :, cells_x] = jnp.zeros_like(ylo[:, :, cells_x])

    @pl.when(jnp.logical_not(corner_dr))
    def _():
        yhi[:, :, 0] = jnp.zeros_like(yhi[:, :, 0])

    row_first[...] = jnp.zeros_like(row_first)
    row_last[...] = jnp.zeros_like(row_last)

    for copy in loads[:4]:
        copy.wait()

    for f in range(fields):
        for c in range(3):
            for x in range(cells_x):
                row_first[0, c, x, f : f + 1, :] = now[f, c, x, 0:1, :]
                row_last[0, c, x, f : f + 1, :] = now[f, c, x, cells_y - 1 : cells_y, :]
    for x in range(cells_x):
        mod_send[x : x + 1] = lame[x + 1, cells_y - 1 : cells_y, :]
        mod_send[cells_x + x : cells_x + x + 1] = shear[x + 1, cells_y - 1 : cells_y, :]

    start(first_rows[2:])
    start(first_moduli[2:])
    start(first_rows[:2])
    start(first_rest)

    for copy in loads[4:]:
        copy.wait()

    for f in range(fields):
        master = f == receivers
        cells[f] = master_cell[0] if master else receiver_cell_s[f]
        lag = master_lag[0] if master else receiver_lag_s[f]
        for k in range(STEPS):
            for c in range(3):
                spot = (f * STEPS + k) * 3 + c
                amps[spot] = master_trace_s[c, lag + k] if master else receiver_trace_s[c, f, lag + k]

    row_at = lax.broadcasted_iota(jnp.int32, (cells_y, depth), 0)
    lane_at = lax.broadcasted_iota(jnp.int32, (cells_y, depth), 1)
    flat_at = row_at * depth + lane_at
    top = row_at == 0
    bottom = row_at == cells_y - 1
    front = lane_at == 0
    back = lane_at == depth - 1
    plane_cells = cells_y * count_y * depth
    first_cell = gx * cells_x * plane_cells + gy * cells_y * depth

    def next_z(v):
        return jnp.where(back, 0.0, pltpu.roll(v, depth - 1, 1))

    def last_z(v):
        return jnp.where(front, 0.0, pltpu.roll(v, 1, 1))

    def next_y(v, row):
        return jnp.where(bottom, row, pltpu.roll(v, cells_y - 1, 0))

    def last_y(v, row):
        return jnp.where(top, row, pltpu.roll(v, 1, 0))

    def wall(k):
        for x in range(cells_x):
            here = [ylo[k, c, x] for c in range(3)]
            beside = [ylo[k, c, x + 1] for c in range(3)]
            above = [row_first[k, c, x] for c in range(3)]
            lam = mod_recv[x : x + 1]
            mu = mod_recv[cells_x + x : cells_x + x + 1]
            grad_y = [above[c] - here[c] for c in range(3)]
            xy = grad_y[0] + (beside[1] - here[1])
            yz = (next_z(here[1]) - here[1]) + grad_y[2]
            dilation = (beside[0] - here[0]) + grad_y[1] + (next_z(here[2]) - here[2])
            low_stress[k, 0, x] = mu * xy
            low_stress[k, 1, x] = lam * dilation + 2.0 * mu * grad_y[1]
            low_stress[k, 2, x] = mu * yz

    def step(k, f, state, earlier, put):
        one = slice(f, f + 1)

        def row(c, x):
            return yhi[k, c, x + 1, one, :]

        here = [xlo[k, f, c] for c in range(3)]
        lam = lame[0]
        mu = shear[0]
        after = [state[f, c, 0] for c in range(3)]
        across = [next_y(here[c], row(c, -1)) for c in range(2)]
        along = [next_z(here[c]) for c in (0, 2)]
        xx = after[0] - here[0]
        dilation = xx + (across[1] - here[1]) + (along[1] - here[2])
        low = [
            lam * dilation + 2.0 * mu * xx,
            mu * ((across[0] - here[0]) + (after[1] - here[1])),
            mu * ((along[0] - here[0]) + (after[2] - here[2])),
        ]
        cell = cells[f]
        amp = [amps[(f * STEPS + k) * 3 + c] for c in range(3)]
        for x in range(cells_x):
            here = after
            after = [state[f, c, x + 1] if x < last else xhi[k, f, c] for c in range(3)]
            lam = lame[x + 1]
            mu = shear[x + 1]
            twice = 2.0 * mu
            gx_ = [after[c] - here[c] for c in range(3)]
            if k == 0:
                turns = [turned_now[f, c, x] for c in range(3)]
                gz_ = [along_now[f, c, x] for c in range(3)]
            else:
                turns = [pltpu.roll(here[c], cells_y - 1, 0) for c in range(3)]
                gz_ = [next_z(here[c]) - here[c] for c in range(3)]
            gy_ = [jnp.where(bottom, row(c, x), turns[c]) - here[c] for c in range(3)]
            spread = lam * (gx_[0] + gy_[1] + gz_[2])
            xx = spread + twice * gx_[0]
            yy = spread + twice * gy_[1]
            zz = spread + twice * gz_[2]
            xy = mu * (gy_[0] + gx_[1])
            xz = mu * (gz_[0] + gx_[2])
            yz = mu * (gz_[1] + gy_[2])
            wall_xy, wall_yy, wall_yz = [low_stress[k, j, x, one, :] for j in range(3)]
            force = [
                (xx - low[0]) + (xy - last_y(xy, wall_xy)) + (xz - last_z(xz)),
                (xy - low[1]) + (yy - last_y(yy, wall_yy)) + (yz - last_z(yz)),
                (xz - low[2]) + (yz - last_y(yz, wall_yz)) + (zz - last_z(zz)),
            ]
            low = [xx, xy, xz]
            placed = flat_at == cell - (first_cell + x * plane_cells)
            scaled = time_step_sq * buoy[x]
            for c in range(3):
                moved = force[c] + jnp.where(placed, amp[c], 0.0)
                put(f, c, x, 2.0 * here[c] - earlier[f, c, x] + scaled * moved)

    def prepare(planes):
        along = [[next_z(v) - v for v in plane] for plane in planes]
        turned = [[pltpu.roll(v, cells_y - 1, 0) for v in plane] for plane in planes]
        return planes, along, turned

    def strain(prepared, far, rows):
        planes, along, turned = prepared
        for x in range(cells_x):
            here = planes[x]
            after = planes[x + 1] if x < last else far
            gx_ = [after[c] - here[c] for c in range(3)]
            gy_ = [jnp.where(bottom, rows[x][c], turned[x][c]) - here[c] for c in range(3)]
            gz_ = along[x]
            yield (
                gx_[0],
                gy_[1],
                gz_[2],
                gy_[0] + gx_[1],
                gz_[0] + gx_[2],
                gz_[1] + gy_[2],
            )

    def summed(load):
        total = load(0)
        for f in range(1, receivers):
            total = total + load(f)
        return total

    def blocks(state):
        whole = [
            [summed(lambda f: state[f, c, x]) for c in range(3)] for x in range(cells_x)
        ]
        master = [[state[receivers, c, x] for c in range(3)] for x in range(cells_x)]
        return prepare(whole), prepare(master)

    def correlate(k, whole, master):
        whole_far = [summed(lambda f: xhi[k, f, c]) for c in range(3)]
        master_far = [xhi[k, receivers, c] for c in range(3)]
        whole_rows = [
            [summed(lambda f: yhi[k, c, x + 1, f : f + 1, :]) for c in range(3)]
            for x in range(cells_x)
        ]
        master_rows = [
            [yhi[k, c, x + 1, receivers : receivers + 1, :] for c in range(3)]
            for x in range(cells_x)
        ]
        pairs = zip(
            strain(whole, whole_far, whole_rows), strain(master, master_far, master_rows)
        )
        for x, (a, b) in enumerate(pairs):
            swell = (a[0] + a[1] + a[2]) * (b[0] + b[1] + b[2])
            twist = 2.0 * (a[0] * b[0] + a[1] * b[1] + a[2] * b[2])
            twist = twist + (a[3] * b[3] + a[4] * b[4] + a[5] * b[5])
            if k == 0:
                totals[0, x] = swell
                totals[1, x] = twist
            else:
                totals[0, x] += swell
                totals[1, x] += twist

    for f in range(fields):
        for c in range(3):
            for x in range(cells_x):
                value = now[f, c, x]
                turned_now[f, c, x] = pltpu.roll(value, cells_y - 1, 0)
                along_now[f, c, x] = next_z(value) - value

    arrive(first_moduli)
    arrive(first_rows)
    wall(0)
    arrive(first_x)

    def put_mid(f, c, x, value):
        mid[f, c, x] = value
        row_first[1, c, x, f : f + 1, :] = value[0:1]
        row_last[1, c, x, f : f + 1, :] = mid[f, c, x, cells_y - 1 : cells_y, :]

    for f in range(split):
        step(0, f, now, prev, put_mid)
    second_x = [
        (remote(mid.at[group, :, 0], xhi.at[1, group], down), has_down, has_up),
        (remote(mid.at[group, :, last], xlo.at[1, group], up), has_up, has_down),
    ]
    start(second_x)
    arrive(first_rest)
    for f in range(split, fields):
        step(0, f, now, prev, put_mid)
    second_rest = [
        (remote(mid.at[rest_all, :, 0], xhi.at[1, rest_all], down), has_down, has_up),
        (remote(mid.at[rest_all, :, last], xlo.at[1, rest_all], up), has_up, has_down),
    ]
    second_rows = rows(1)
    start(second_rows[2:])
    start(second_rest)
    start(second_rows[:2])
    second_round = second_x + second_rest + second_rows
    uppers = [second_x[0], second_rest[0], second_rows[2]]
    others = [second_x[1], second_rest[1], second_rows[0], second_rows[1], second_rows[3]]
    correlate(0, *blocks(now))
    ready = blocks(mid)
    arrive(uppers)
    correlate(1, *ready)

    share = depth // groups
    lane_part = lane_at // share
    for g in range(groups):
        for j in range(2):
            packed = None
            for x in range(cells_x):
                turn = (share * (x - g)) % depth
                piece = totals[j, x] if turn == 0 else pltpu.roll(totals[j, x], turn, 1)
                packed = piece if packed is None else jnp.where(lane_part == x, piece, packed)
            share_send[g, j] = packed
    third_round = [
        (remote(share_send.at[peers[d][0]], share_recv.at[d], peers[d]), True, True)
        for d in range(groups - 1)
    ]
    for copy, _, _ in third_round:
        copy.start()

    def put_out(f, c, x, value):
        adj_out[f, c, x] = value

    arrive(others)
    wall(1)
    for f in range(receivers):
        step(1, f, mid, now, put_out)

    for copy, _, _ in third_round:
        copy.wait_recv()
    scale_out = 1.0 / (STEPS * receivers * groups)
    for j in range(2):
        part = share_send[grp, j]
        for d in range(groups - 1):
            part = part + share_recv[d, j]
        part = part * scale_out
        for x in range(cells_x):
            piece = part if x == 0 else pltpu.roll(part, depth - share * x, 1)
            kern_out[j, x] = piece[:, 0:share]
    sent(first_x + first_moduli + first_rest + first_rows)
    sent(second_round)
    for copy, _, _ in third_round:
        copy.wait_send()


def hand_over(adj_made, kern_made, adj_out, kern_out, sems):
    adj_copy = pltpu.make_async_copy(adj_made, adj_out, sems.at[0])
    kern_copy = pltpu.make_async_copy(kern_made, kern_out, sems.at[1])
    adj_copy.start()
    kern_copy.start()
    adj_copy.wait()
    kern_copy.wait()


def local(
    fwd_now,
    fwd_prev,
    adj_now,
    adj_prev,
    lame_first,
    shear_mod,
    buoyancy,
    master_cell,
    master_lag,
    master_trace,
    receiver_cell,
    receiver_lag,
    receiver_trace,
):
    cells_x, cells_y, depth = lame_first.shape
    receivers = adj_now.shape[0]
    fields = receivers + 1
    sizes = tuple(lax.axis_size(axis) for axis in ("grp", "gx", "gy"))
    groups = sizes[0]
    lanes = -(-fields // 8) * 8
    block = (fields, 3, cells_x, cells_y, depth)
    scalar = pl.BlockSpec(memory_space=pltpu.SMEM)
    whole = pl.BlockSpec(memory_space=pltpu.HBM)
    vector = pl.BlockSpec(memory_space=pltpu.VMEM)

    def room(*shape):
        return pltpu.VMEM(shape, jnp.float32)

    def stay(value):
        return pltpu.with_memory_space_constraint(value, pltpu.HBM)

    made = pl.pallas_call(
        functools.partial(kernel, sizes),
        out_shape=(
            pltpu.VMEM(adj_now.shape, jnp.float32),
            pltpu.VMEM((2, cells_x, cells_y, depth // groups), jnp.float32),
        ),
        in_specs=[scalar] * 2 + [whole] * 11,
        out_specs=(vector, vector),
        scratch_shapes=[
            room(*block),
            room(*block),
            room(*block),
            room(cells_x + 1, cells_y, depth),
            room(cells_x + 1, cells_y, depth),
            room(cells_x, cells_y, depth),
            room(STEPS, fields, 3, cells_y, depth),
            room(STEPS, fields, 3, cells_y, depth),
            room(STEPS, 3, cells_x + 1, lanes, depth),
            room(STEPS, 3, cells_x + 1, lanes, depth),
            room(STEPS, 3, cells_x, lanes, depth),
            room(STEPS, 3, cells_x, lanes, depth),
            room(2 * cells_x, depth),
            room(2 * cells_x, depth),
            room(STEPS, 3, cells_x, lanes, depth),
            room(*block),
            room(*block),
            room(2, cells_x, cells_y, depth),
            room(groups, 2, cells_y, depth),
            room(groups - 1, 2, cells_y, depth),
            pltpu.SMEM((fields,), jnp.int32),
            pltpu.SMEM((fields * STEPS * 3,), jnp.float32),
            pltpu.SMEM((3,) + master_trace.shape[:1], jnp.float32),
            pltpu.SMEM((receivers,), jnp.int32),
            pltpu.SMEM((receivers,), jnp.int32),
            pltpu.SMEM((3,) + receiver_trace.shape[:2], jnp.float32),
            pltpu.SemaphoreType.DMA((11,)),
            pltpu.SemaphoreType.DMA((32,)),
            pltpu.SemaphoreType.DMA((32,)),
        ],
        compiler_params=pltpu.CompilerParams(
            collective_id=0, has_side_effects=True, vmem_limit_bytes=32 * 1024 * 1024
        ),
    )(
        master_cell,
        master_lag,
        stay(master_trace.T),
        stay(receiver_cell),
        stay(receiver_lag),
        stay(receiver_trace.transpose(2, 0, 1)),
        stay(fwd_now),
        stay(fwd_prev),
        stay(adj_now),
        stay(adj_prev),
        stay(lame_first),
        stay(shear_mod),
        stay(buoyancy),
    )
    made = [pltpu.with_memory_space_constraint(value, pltpu.VMEM) for value in made]
    return pl.pallas_call(
        hand_over,
        out_shape=tuple(jax.ShapeDtypeStruct(value.shape, value.dtype) for value in made),
        in_specs=[pl.BlockSpec(memory_space=pltpu.VMEM)] * 2,
        out_specs=(whole, whole),
        scratch_shapes=[pltpu.SemaphoreType.DMA((2,))],
    )(*made)


def solution(mesh):
    in_specs = (
        P(None, "gx", "gy", None),
        P(None, "gx", "gy", None),
        P("grp", None, "gx", "gy", None),
        P("grp", None, "gx", "gy", None),
        P("gx", "gy", None),
        P("gx", "gy", None),
        P("gx", "gy", None),
        P(),
        P(),
        P(),
        P("grp"),
        P("grp"),
        P("grp", None, None),
    )
    out_specs = (P("grp", None, "gx", "gy", None), P(None, "gx", "gy", "grp"))
    return jax.shard_map(local, mesh=mesh, in_specs=in_specs, out_specs=out_specs, check_vma=False)
```
